256 devices in a mesh: seq: 64 (over z, y, core), head: 4 (over x).
Axes of the slice: x: 4, y: 4, z: 8, core: 2. Of those that a mesh axis runs over, the one named last changes fastest.
Arguments:
- video_q: bfloat16 [16384, 3072], P('seq', 'head'), may hold values from -200 to 200
- video_k: bfloat16 [16384, 3072], P('seq', 'head'), may hold values from -200 to 200
- video_v: bfloat16 [16384, 3072], P('seq', 'head'), may hold values from -6 to 6
- audio_q: bfloat16 [16384, 3072], P('seq', 'head'), may hold values from -200 to 200
- audio_k: bfloat16 [16384, 3072], P('seq', 'head'), may hold values from -200 to 200
- audio_v: bfloat16 [16384, 3072], P('seq', 'head'), may hold values from -6 to 6
- video_q_gain: float32 [3072], P('head'), may hold values from 0.1 to 1.9
- audio_k_gain: float32 [3072], P('head'), may hold values from 0.1 to 1.9
- audio_q_gain: float32 [3072], P('head'), may hold values from 0.1 to 1.9
- video_k_gain: float32 [3072], P('head'), may hold values from 0.1 to 1.9
- tile_first: int32 [64], replicated, may hold values from 0 to 63, as said below
- tile_count: int32 [64], replicated, may hold values from 1 to 5
Outputs:
- video_out: bfloat16 [16384, 3072], P('seq', 'head')
- audio_out: bfloat16 [16384, 3072], P('seq', 'head')
The draws below stay inside these ranges and needn't reach their ends.
Inputs may be any that keep to these rules, and one draw needn't show every extreme that they name: Stretch c intersects tiles tile_first[c] .. tile_first[c] + tile_count[c] - 1, which include tile c and lie within c - 2 .. c + 2.
All inputs are finite; a program needn't handle non-finite values.
Results may differ from the reference program's by a relative error of at most 0.017.
Values may be sent and summed in bfloat16 or wider, within the bound.
A program may use at most 64 MiB of HBM per device.

```python
import math
import jax
import jax.numpy as jnp
from jax import lax

HEADS = 24
HEAD_DIM = 128
D = 3072
TOK_V = 256
TOK_A = 256
REACH = 2
STRETCHES = 64
TOKENS_V = 16384
TOKENS_A = 16384


def textured(entries, key, rows, cols):
    row_key, col_key = jax.random.split(key)
    row_scale = jnp.exp(jax.random.uniform(row_key, (rows, 1), jnp.float32, 0.0, math.log(10.0))) / math.sqrt(10.0)
    col_scale = jnp.exp(jax.random.uniform(col_key, (1, cols), jnp.float32, 0.0, math.log(10.0))) / math.sqrt(10.0)
    return entries * row_scale * col_scale


def background(key, rows, cols):
    entries = jax.random.truncated_normal(key, -6.0, 6.0, (rows, cols), jnp.float32)
    return textured(entries, jax.random.fold_in(key, 9), rows, cols)


def draw_video_q(key, part):
    key = jax.random.fold_in(key, 1)
    base = background(key, TOKENS_V, D)
    return base.astype(jnp.bfloat16)


def draw_audio_k(key, part):
    key = jax.random.fold_in(key, 2)
    base = background(key, TOKENS_A, D)
    return base.astype(jnp.bfloat16)


def draw_audio_q(key, part):
    key = jax.random.fold_in(key, 3)
    base = background(key, TOKENS_A, D)
    return base.astype(jnp.bfloat16)


def draw_video_k(key, part):
    key = jax.random.fold_in(key, 4)
    base = background(key, TOKENS_V, D)
    return base.astype(jnp.bfloat16)


def windows(key):
    key = jax.random.fold_in(key, 7)
    below_key, above_key = jax.random.split(key)
    below = jax.random.randint(below_key, (STRETCHES,), 0, REACH + 1)
    above = jax.random.randint(above_key, (STRETCHES,), 0, REACH + 1)
    index = jnp.arange(STRETCHES, dtype=jnp.int32)
    middle = index == STRETCHES // 2
    below = jnp.where(middle, REACH, below)
    above = jnp.where(middle, REACH, above)
    below = jnp.where(index == STRETCHES - 1, 0, below)
    first = jnp.maximum(index - below, 0)
    last = jnp.minimum(index + above, STRETCHES - 1)
    return (first.astype(jnp.int32), (last - first + 1).astype(jnp.int32))


def draw_tile_first(key, part):
    first, count = windows(key)
    return first


def draw_tile_count(key, part):
    first, count = windows(key)
    return count


def level_of(stream_key, extent, shards, least, top_value):
    level, own = 1.0, jax.random.fold_in(stream_key, 6)
    for dim, parts in shards:
        draws = jnp.exp(jax.random.uniform(jax.random.fold_in(own, dim), (parts,), jnp.float32, least / len(shards), top_value / len(shards)))
        level = level * jnp.repeat(draws, extent[dim] // parts).reshape([-1 if axis == dim else 1 for axis in range(len(extent))])
    return level


def normal_values(key, dims, width, most, shards=(), held_as=jnp.bfloat16):
    drawn = jax.random.normal(key, dims, jnp.float32) * width
    if len(shards) > 0:
        drawn = level_of(key, dims, shards, -0.22, 0.18) * drawn
    return jnp.clip(drawn, min=-most, max=most).astype(held_as)


def setup_inputs(seed: int = 0) -> dict:
    splits = jax.random.split(jax.random.key(seed), 13)
    return {
        "video_q": draw_video_q(jax.random.fold_in(splits[12], 71), 0),
        "video_k": draw_video_k(jax.random.fold_in(splits[12], 71), 0),
        "video_v": normal_values(splits[2], (TOKENS_V, D), 1.0, 6.0, ((0, 64), (1, 4))),
        "audio_q": draw_audio_q(jax.random.fold_in(splits[12], 71), 0),
        "audio_k": draw_audio_k(jax.random.fold_in(splits[12], 71), 0),
        "audio_v": normal_values(splits[5], (TOKENS_A, D), 1.0, 6.0, ((0, 64), (1, 4))),
        "video_q_gain": jnp.clip(1.0 + 0.18 * jax.random.normal(splits[6], (D,), jnp.float32), 0.1, 1.9),
        "audio_k_gain": jnp.clip(1.0 + 0.18 * jax.random.normal(splits[7], (D,), jnp.float32), 0.1, 1.9),
        "audio_q_gain": jnp.clip(1.0 + 0.18 * jax.random.normal(splits[8], (D,), jnp.float32), 0.1, 1.9),
        "video_k_gain": jnp.clip(1.0 + 0.18 * jax.random.normal(splits[9], (D,), jnp.float32), 0.1, 1.9),
        "tile_first": draw_tile_first(jax.random.fold_in(splits[12], 71), 0),
        "tile_count": draw_tile_count(jax.random.fold_in(splits[12], 71), 0),
    }


EPS = 1e-06
NEG = -1e+30

def normalize(x, gain):
    wide = x.astype(jnp.float32)
    mean_square = lax.optimization_barrier(jnp.sum(wide * wide, axis=1, keepdims=True)) / wide.shape[1]
    return (wide * lax.rsqrt(mean_square + EPS) * gain).astype(jnp.bfloat16)

def attend(query, keys, values, valid):
    rows = query.shape[0]
    length = keys.shape[0]
    qh = query.astype(jnp.float32).reshape(rows, HEADS, HEAD_DIM)
    kh = keys.astype(jnp.float32).reshape(length, HEADS, HEAD_DIM)
    vh = values.astype(jnp.float32).reshape(length, HEADS, HEAD_DIM)
    scores = jnp.einsum('qhe,khe->hqk', qh, kh) * HEAD_DIM ** (-0.5)
    scores = jnp.where(valid[None, None, :], scores, NEG)
    top = lax.optimization_barrier(jnp.max(scores, axis=2, keepdims=True))
    weights = jnp.where(valid[None, None, :], jnp.exp(scores - top), 0.0)
    total = lax.optimization_barrier(jnp.sum(weights, axis=2))
    rounded = lax.optimization_barrier(weights.astype(jnp.bfloat16)).astype(jnp.float32)
    mixed = jnp.einsum('hqk,khe->qhe', rounded, vh) / jnp.transpose(total)[:, :, None]
    return mixed.reshape(rows, HEADS * HEAD_DIM).astype(jnp.bfloat16)

def reference(video_q, video_k, video_v, audio_q, audio_k, audio_v, video_q_gain, audio_k_gain, audio_q_gain, video_k_gain, tile_first, tile_count):
    nvq = normalize(video_q, video_q_gain)
    nak = normalize(audio_k, audio_k_gain)
    naq = normalize(audio_q, audio_q_gain)
    nvk = normalize(video_k, video_k_gain)
    span = 2 * REACH + 1
    vk_pad = jnp.pad(nvk, ((REACH * TOK_V, REACH * TOK_V), (0, 0)))
    vv_pad = jnp.pad(video_v, ((REACH * TOK_V, REACH * TOK_V), (0, 0)))
    ak_pad = jnp.pad(nak, ((REACH * TOK_A, REACH * TOK_A), (0, 0)))
    av_pad = jnp.pad(audio_v, ((REACH * TOK_A, REACH * TOK_A), (0, 0)))

    def audio_one(stretch):
        query = lax.dynamic_slice_in_dim(naq, stretch * TOK_A, TOK_A, 0)
        keys = lax.dynamic_slice_in_dim(vk_pad, stretch * TOK_V, span * TOK_V, 0)
        values = lax.dynamic_slice_in_dim(vv_pad, stretch * TOK_V, span * TOK_V, 0)
        tile = stretch - REACH + jnp.arange(span * TOK_V).astype(jnp.int32) // TOK_V
        first = tile_first[stretch]
        valid = (tile >= 0) & (tile < STRETCHES) & (tile >= first) & (tile < first + tile_count[stretch])
        return attend(query, keys, values, valid)

    def video_one(tile):
        query = lax.dynamic_slice_in_dim(nvq, tile * TOK_V, TOK_V, 0)
        keys = lax.dynamic_slice_in_dim(ak_pad, tile * TOK_A, span * TOK_A, 0)
        values = lax.dynamic_slice_in_dim(av_pad, tile * TOK_A, span * TOK_A, 0)
        stretch = tile - REACH + jnp.arange(span * TOK_A).astype(jnp.int32) // TOK_A
        safe = jnp.clip(stretch, 0, STRETCHES - 1)
        first = tile_first[safe]
        valid = (stretch >= 0) & (stretch < STRETCHES) & (tile >= first) & (tile < first + tile_count[safe])
        return attend(query, keys, values, valid)
    index = jnp.arange(STRETCHES).astype(jnp.int32)
    audio_out = lax.map(audio_one, index).reshape(TOKENS_A, D)
    video_out = lax.map(video_one, index).reshape(TOKENS_V, D)
    return (video_out, audio_out)
```

```python
import jax
import jax.numpy as jnp
from jax import lax
from jax.experimental import pallas as pl
from jax.experimental.pallas import tpu as pltpu
from jax.sharding import PartitionSpec as P

HEAD_DIM = 128
EPS = 1e-06
NEG = -1e30
MESH = pl.DeviceIdType.MESH
LOG2E = 1.4426950408889634

PARTNER, DIRECT, NEAR, FAR = 0, 1, 2, 3
OFFSET = (1, -2, -1, 2)
AUDIO, VIDEO = 0, 1


def kernel(
    count_seq,
    count_head,
    vq_hbm,
    vk_hbm,
    vv_hbm,
    aq_hbm,
    ak_hbm,
    av_hbm,
    vqg,
    akg,
    aqg,
    vkg,
    first_ref,
    count_ref,
    vout,
    aout,
    raw,
    own_v,
    nq,
    nk,
    far_k,
    far_v,
    sums,
    sums_in,
    local_sem,
    sum_send,
    sum_recv,
    v_send,
    v_recv,
    k_send,
    k_recv,
):
    seq = lax.axis_index("seq")
    head = lax.axis_index("head")
    sigma = 1 - 2 * lax.rem(seq, 2)
    heads = nk.shape[1]
    rows = raw.shape[1]
    width = raw.shape[2] * count_head

    def at(by):
        return lax.rem(seq + by * sigma + count_seq, count_seq)

    loads = []
    for i, ref in enumerate((ak_hbm, vk_hbm, vq_hbm, aq_hbm)):
        loads.append(pltpu.make_async_copy(ref, raw.at[i], local_sem.at[i]))
    for i, ref in enumerate((av_hbm, vv_hbm)):
        loads.append(pltpu.make_async_copy(ref, own_v.at[i], local_sem.at[4 + i]))
    for load in loads:
        load.start()

    barrier = pltpu.get_barrier_semaphore()
    for by in (1, 2, -1, -2):
        pl.semaphore_signal(barrier, inc=1, device_id=(at(by), head), device_id_type=MESH)
    for by in range(1, count_head):
        pl.semaphore_signal(
            barrier, inc=1, device_id=(seq, lax.rem(head + by, count_head)), device_id_type=MESH
        )
    pl.semaphore_wait(barrier, 4 + count_head - 1)

    def target(slot, mod):
        if (slot, mod) in ((FAR, AUDIO), (NEAR, VIDEO)):
            return at(1)
        return at({PARTNER: 1, DIRECT: 2, NEAR: -1, FAR: -2}[slot])

    def v_copy(slot, mod):
        if (slot, mod) == (FAR, AUDIO):
            src = far_v.at[NEAR, AUDIO]
        elif (slot, mod) == (NEAR, VIDEO):
            src = far_v.at[FAR, VIDEO]
        else:
            src = (av_hbm, vv_hbm)[mod]
        return pltpu.make_async_remote_copy(
            src_ref=src,
            dst_ref=far_v.at[slot, mod],
            send_sem=v_send.at[slot, mod],
            recv_sem=v_recv.at[slot, mod],
            device_id=(target(slot, mod), head),
            device_id_type=MESH,
        )

    def k_copy(slot, mod, h):
        if (slot, mod) == (FAR, AUDIO):
            src = far_k.at[NEAR, AUDIO, h]
        elif (slot, mod) == (NEAR, VIDEO):
            src = far_k.at[FAR, VIDEO, h]
        else:
            src = nk.at[mod, h]
        return pltpu.make_async_remote_copy(
            src_ref=src,
            dst_ref=far_k.at[slot, mod, h],
            send_sem=k_send.at[slot, mod, h],
            recv_sem=k_recv.at[slot, mod, h],
            device_id=(target(slot, mod), head),
            device_id_type=MESH,
        )

    sends = ((NEAR, AUDIO), (FAR, VIDEO), (DIRECT, AUDIO), (DIRECT, VIDEO), (PARTNER, AUDIO), (PARTNER, VIDEO))
    relays = ((FAR, AUDIO), (NEAR, VIDEO))
    for slot, mod in sends:
        v_copy(slot, mod).start()

    lane = lax.broadcasted_iota(jnp.int32, (rows, HEAD_DIM), 1)
    packed = jnp.zeros((rows, HEAD_DIM), jnp.float32)
    for i in range(4):
        loads[i].wait()
        total = jnp.zeros((rows, HEAD_DIM), jnp.float32)
        for h in range(heads):
            wide = raw[i, :, h * HEAD_DIM : (h + 1) * HEAD_DIM].astype(jnp.float32)
            total += wide * wide
        packed = jnp.where(lane == i, jnp.sum(total, axis=1, keepdims=True), packed)
    sums[...] = jnp.transpose(packed)[:8]

    def sum_copy(by):
        return pltpu.make_async_remote_copy(
            src_ref=sums,
            dst_ref=sums_in.at[by - 1],
            send_sem=sum_send.at[by - 1],
            recv_sem=sum_recv.at[by - 1],
            device_id=(seq, lax.rem(head + by, count_head)),
            device_id_type=MESH,
        )

    for by in range(1, count_head):
        sum_copy(by).start()
    all_sums = sums[...]
    for by in range(1, count_head):
        sum_copy(by).wait_recv()
        all_sums += sums_in[by - 1]
    scale = lax.rsqrt(all_sums / width + EPS)
    scale = jnp.transpose(jnp.concatenate([scale] * (HEAD_DIM // 8), axis=0))

    def normalized(i, gain, h):
        cols = slice(h * HEAD_DIM, (h + 1) * HEAD_DIM)
        wide = raw[i, :, cols].astype(jnp.float32)
        return (wide * scale[:, i : i + 1] * gain[cols]).astype(jnp.bfloat16)

    for h in range(heads):
        nk[AUDIO, h] = normalized(0, akg, h)
        nk[VIDEO, h] = normalized(1, vkg, h)
        for slot, mod in sends:
            k_copy(slot, mod, h).start()
    for h in range(heads):
        nq[VIDEO, h] = normalized(2, vqg, h)
        nq[AUDIO, h] = normalized(3, aqg, h)
    loads[4].wait()
    loads[5].wait()

    def covers(stretch, tile):
        safe = lax.rem(stretch + count_seq, count_seq)
        first = first_ref[safe]
        inside = (stretch >= 0) & (stretch < count_seq) & (tile >= 0) & (tile < count_seq)
        return inside & (tile >= first) & (tile < first + count_ref[safe])

    bias = ([], [])
    for slot in range(4):
        other = seq + OFFSET[slot] * sigma
        bias[VIDEO].append(jnp.where(covers(other, seq), 0.0, NEG))
        bias[AUDIO].append(jnp.where(covers(seq, other), 0.0, NEG))

    factor = LOG2E * HEAD_DIM**-0.5

    def attend(q_mod, h):
        k_mod = 1 - q_mod
        cols = pl.ds(pl.multiple_of(h * HEAD_DIM, HEAD_DIM), HEAD_DIM)
        query = nq[q_mod, h]
        keys = [nk[k_mod, h]] + [far_k[slot, k_mod, h] for slot in range(4)]
        values = [own_v[k_mod, :, cols]] + [far_v[slot, k_mod, :, cols] for slot in range(4)]
        off = [0.0] + bias[q_mod]
        scores, top = [], None
        for key, add in zip(keys, off):
            score = lax.dot_general(
                query, key, (((1,), (1,)), ((), ())), preferred_element_type=jnp.float32
            )
            scores.append(score)
            most = jnp.max(score, axis=1, keepdims=True) + add
            top = most if top is None else jnp.maximum(top, most)
        total = jnp.zeros((rows, 1), jnp.float32)
        mixed = jnp.zeros((rows, HEAD_DIM), jnp.float32)
        for score, value, add in zip(scores, values, off):
            weights = jnp.exp2((score - (top - add)) * factor)
            total += jnp.sum(weights, axis=1, keepdims=True)
            mixed += jnp.dot(
                weights.astype(jnp.bfloat16), value, preferred_element_type=jnp.float32
            )
        return (mixed / total).astype(jnp.bfloat16), cols

    for slot, mod in ((NEAR, AUDIO), (FAR, VIDEO)):
        v_copy(slot, mod).wait_recv()
    for slot, mod in relays:
        v_copy(slot, mod).start()
    for slot, mod in ((PARTNER, AUDIO), (PARTNER, VIDEO), (DIRECT, AUDIO), (DIRECT, VIDEO)) + relays:
        v_copy(slot, mod).wait_recv()

    def forward(h):
        for slot, mod in ((NEAR, AUDIO), (FAR, VIDEO)):
            k_copy(slot, mod, h).wait_recv()
        for slot, mod in relays:
            k_copy(slot, mod, h).start()

    forward(0)

    def body(h, carry):
        @pl.when(h < heads - 1)
        def _():
            forward(h + 1)

        for slot, mod in ((PARTNER, AUDIO), (PARTNER, VIDEO), (DIRECT, AUDIO), (DIRECT, VIDEO)) + relays:
            k_copy(slot, mod, h).wait_recv()
        result, cols = attend(VIDEO, h)
        vout[:, cols] = result
        result, cols = attend(AUDIO, h)
        aout[:, cols] = result
        return carry

    lax.fori_loop(0, heads, body, 0)

    for by in range(1, count_head):
        sum_copy(by).wait_send()
    for slot, mod in sends + relays:
        v_copy(slot, mod).wait_send()

    def drain(h, carry):
        for slot, mod in sends + relays:
            k_copy(slot, mod, h).wait_send()
        return carry

    lax.fori_loop(0, heads, drain, 0)


def local(
    video_q,
    video_k,
    video_v,
    audio_q,
    audio_k,
    audio_v,
    video_q_gain,
    audio_k_gain,
    audio_q_gain,
    video_k_gain,
    tile_first,
    tile_count,
):
    count_seq, count_head = lax.axis_size("seq"), lax.axis_size("head")
    rows, cols = video_q.shape
    heads = cols // HEAD_DIM
    gains = (video_q_gain, audio_k_gain, audio_q_gain, video_k_gain)

    def body(*refs):
        kernel(count_seq, count_head, *refs)

    hbm = pl.BlockSpec(memory_space=pl.ANY)
    vmem = pl.BlockSpec(memory_space=pltpu.VMEM)
    smem = pl.BlockSpec(memory_space=pltpu.SMEM)
    return pl.pallas_call(
        body,
        out_shape=(
            jax.ShapeDtypeStruct((rows, cols), jnp.bfloat16),
            jax.ShapeDtypeStruct((rows, cols), jnp.bfloat16),
        ),
        in_specs=[hbm] * 6 + [vmem] * 4 + [smem] * 2,
        out_specs=(vmem, vmem),
        scratch_shapes=[
            pltpu.VMEM((4, rows, cols), jnp.bfloat16),
            pltpu.VMEM((2, rows, cols), jnp.bfloat16),
            pltpu.VMEM((2, heads, rows, HEAD_DIM), jnp.bfloat16),
            pltpu.VMEM((2, heads, rows, HEAD_DIM), jnp.bfloat16),
            pltpu.VMEM((4, 2, heads, rows, HEAD_DIM), jnp.bfloat16),
            pltpu.VMEM((4, 2, rows, cols), jnp.bfloat16),
            pltpu.VMEM((8, rows), jnp.float32),
            pltpu.VMEM((count_head - 1, 8, rows), jnp.float32),
            pltpu.SemaphoreType.DMA((6,)),
            pltpu.SemaphoreType.DMA((count_head - 1,)),
            pltpu.SemaphoreType.DMA((count_head - 1,)),
            pltpu.SemaphoreType.DMA((4, 2)),
            pltpu.SemaphoreType.DMA((4, 2)),
            pltpu.SemaphoreType.DMA((4, 2, heads)),
            pltpu.SemaphoreType.DMA((4, 2, heads)),
        ],
        compiler_params=pltpu.CompilerParams(
            collective_id=0, has_side_effects=True, vmem_limit_bytes=56 * 1024 * 1024
        ),
        name="attend",
    )(video_q, video_k, video_v, audio_q, audio_k, audio_v, *gains, tile_first, tile_count)


def solution(mesh):
    return jax.shard_map(
        local,
        mesh=mesh,
        in_specs=(P("seq", "head"),) * 6 + (P("head"),) * 4 + (P(), P()),
        out_specs=(P("seq", "head"), P("seq", "head")),
        check_vma=False,
    )
```

```python
import jax
import jax.numpy as jnp
from jax import lax
from jax.experimental import pallas as pl
from jax.experimental.pallas import tpu as pltpu
from jax.sharding import PartitionSpec as P

HEAD_DIM = 128
EPS = 1e-06
NEG = -1e30
MESH = pl.DeviceIdType.MESH
LOG2E = 1.4426950408889634
FACTOR = LOG2E * HEAD_DIM**-0.5

PARTNER, DIRECT, NEAR, FAR = 0, 1, 2, 3
OFFSET = (1, -2, -1, 2)
AUDIO, VIDEO = 0, 1
KEY, VALUE = 0, 1
SPLIT = ((NEAR, AUDIO), (FAR, VIDEO))
RELAY = ((FAR, AUDIO), (NEAR, VIDEO))


def kernel(
    count_seq,
    count_head,
    vq_hbm,
    vk_hbm,
    vv_hbm,
    aq_hbm,
    ak_hbm,
    av_hbm,
    vqg,
    akg,
    aqg,
    vkg,
    first_ref,
    count_ref,
    vout,
    aout,
    raw,
    raw_v,
    own,
    nq,
    far,
    top_ref,
    total_ref,
    mixed_ref,
    sums,
    sums_in,
    local_sem,
    value_sem,
    sum_send,
    sum_recv,
    partner_send,
    partner_recv,
    split_send,
    split_recv,
    relay_send,
    relay_recv,
    direct_send,
    direct_recv,
):
    seq = lax.axis_index("seq")
    head = lax.axis_index("head")
    sigma = 1 - 2 * lax.rem(seq, 2)
    heads = nq.shape[0]
    rows = raw.shape[1]
    width = raw.shape[2] * count_head
    behind = (seq - sigma >= 0) & (seq - sigma < count_seq)
    ahead = (seq + 2 * sigma >= 0) & (seq + 2 * sigma < count_seq)

    loads = []
    for i, ref in enumerate((ak_hbm, vk_hbm, vq_hbm, aq_hbm)):
        loads.append(pltpu.make_async_copy(ref, raw.at[i], local_sem.at[i]))
    value_loads = []
    for mod, ref in enumerate((av_hbm, vv_hbm)):
        for h in range(heads):
            value_loads.append(
                pltpu.make_async_copy(
                    ref.at[:, pl.ds(h * HEAD_DIM, HEAD_DIM)],
                    raw_v.at[h, mod],
                    value_sem.at[mod, h],
                )
            )
    barrier = pltpu.get_barrier_semaphore()

    def greet(by):
        pl.semaphore_signal(barrier, inc=1, device_id=(seq + by * sigma, head), device_id_type=MESH)

    greet(1)
    for by in range(1, count_head):
        pl.semaphore_signal(
            barrier, inc=1, device_id=(seq, lax.rem(head + by, count_head)), device_id_type=MESH
        )

    @pl.when(behind)
    def _():
        greet(-1)
        greet(-2)

    @pl.when(ahead)
    def _():
        greet(2)

    for load in value_loads + loads:
        load.start()
    for load in value_loads:
        load.wait()
    for h in range(heads):
        for mod in (AUDIO, VIDEO):
            for r in range(0, rows, HEAD_DIM):
                own[h, mod, VALUE, r : r + HEAD_DIM] = jnp.transpose(raw_v[h, mod, r : r + HEAD_DIM])
    peers = count_head + 2 * behind.astype(jnp.int32) + ahead.astype(jnp.int32)
    pl.semaphore_wait(barrier, peers)

    def remote(src, dst, send, recv, by):
        return pltpu.make_async_remote_copy(
            src_ref=src,
            dst_ref=dst,
            send_sem=send,
            recv_sem=recv,
            device_id=(seq + by * sigma, head),
            device_id_type=MESH,
        )

    def block(ref, mod, part):
        if isinstance(part, int) and part == 0:
            return ref.at[:, mod, VALUE]
        return ref.at[part - 1, mod, KEY]

    def split_copy(slot, mod, part):
        by = -1 if slot == NEAR else -2
        return remote(
            block(own, mod, part),
            block(far.at[slot], mod, part),
            split_send.at[mod, part],
            split_recv.at[mod, part],
            by,
        )

    def relay_copy(slot, mod, part):
        held = NEAR if slot == FAR else FAR
        return remote(
            block(far.at[held], mod, part),
            block(far.at[slot], mod, part),
            relay_send.at[mod, part],
            relay_recv.at[mod, part],
            1,
        )

    def partner_copy(kv):
        return remote(own.at[:, :, kv], far.at[PARTNER, :, :, kv], partner_send.at[kv], partner_recv.at[kv], 1)

    def direct_copy(h):
        return remote(own.at[h], far.at[DIRECT, h], direct_send.at[h], direct_recv.at[h], 2)

    def start_split(part):
        @pl.when(behind)
        def _():
            for slot, mod in SPLIT:
                split_copy(slot, mod, part).start()

    def start_relay(part):
        @pl.when(behind)
        def _():
            split_copy(NEAR, AUDIO, part).wait_recv()
            relay_copy(FAR, AUDIO, part).start()

        @pl.when(ahead)
        def _():
            split_copy(FAR, VIDEO, part).wait_recv()
            relay_copy(NEAR, VIDEO, part).start()

    def finish_relay(part):
        @pl.when(ahead)
        def _():
            relay_copy(FAR, AUDIO, part).wait_recv()

        @pl.when(behind)
        def _():
            relay_copy(NEAR, VIDEO, part).wait_recv()

    start_split(0)
    partner_copy(VALUE).start()

    def clear(slot):
        def body(h, carry):
            far[slot, h] = jnp.zeros(far.shape[2:], far.dtype)
            return carry

        lax.fori_loop(0, heads, body, 0)

    @pl.when(jnp.logical_not(behind))
    def _():
        clear(DIRECT)
        clear(NEAR)

    @pl.when(jnp.logical_not(ahead))
    def _():
        clear(FAR)

    lane = lax.broadcasted_iota(jnp.int32, (rows, HEAD_DIM), 1)
    packed = jnp.zeros((rows, HEAD_DIM), jnp.float32)
    for i in range(4):
        loads[i].wait()
        total = jnp.zeros((rows, HEAD_DIM), jnp.float32)
        for h in range(heads):
            wide = raw[i, :, h * HEAD_DIM : (h + 1) * HEAD_DIM].astype(jnp.float32)
            total += wide * wide
        packed = jnp.where(lane == i, jnp.sum(total, axis=1, keepdims=True), packed)
    sums[...] = jnp.transpose(packed)[:8]

    def sum_copy(by):
        return pltpu.make_async_remote_copy(
            src_ref=sums,
            dst_ref=sums_in.at[by - 1],
            send_sem=sum_send.at[by - 1],
            recv_sem=sum_recv.at[by - 1],
            device_id=(seq, lax.rem(head + by, count_head)),
            device_id_type=MESH,
        )

    for by in range(1, count_head):
        sum_copy(by).start()
    all_sums = sums[...]
    for by in range(1, count_head):
        sum_copy(by).wait_recv()
        all_sums += sums_in[by - 1]
    scale = lax.rsqrt(all_sums / width + EPS)
    scale = jnp.transpose(jnp.concatenate([scale] * (HEAD_DIM // 8), axis=0))

    def normalized(i, gain, h):
        cols = slice(h * HEAD_DIM, (h + 1) * HEAD_DIM)
        wide = raw[i, :, cols].astype(jnp.float32)
        return (wide * scale[:, i : i + 1] * gain[cols]).astype(jnp.bfloat16)

    for h in range(heads):
        own[h, AUDIO, KEY] = normalized(0, akg, h)
        own[h, VIDEO, KEY] = normalized(1, vkg, h)
        start_split(h + 1)

        @pl.when(ahead)
        def _():
            direct_copy(h).start()

    partner_copy(KEY).start()
    for h in range(heads):
        nq[h, VIDEO] = normalized(2, vqg, h)
        nq[h, AUDIO] = normalized(3, aqg, h)

    def covers(stretch, tile):
        safe = lax.rem(stretch + count_seq, count_seq)
        first = first_ref[safe]
        inside = (stretch >= 0) & (stretch < count_seq) & (tile >= 0) & (tile < count_seq)
        return inside & (tile >= first) & (tile < first + count_ref[safe])

    bias = ([], [])
    for slot in range(4):
        other = seq + OFFSET[slot] * sigma
        bias[VIDEO].append(jnp.where(covers(other, seq), 0.0, NEG))
        bias[AUDIO].append(jnp.where(covers(seq, other), 0.0, NEG))

    def attend(h, slots, opening=False, closing=False):
        jobs = []
        for q_mod in (VIDEO, AUDIO):
            refs = [(far.at[slot, h, 1 - q_mod], bias[q_mod][slot]) for slot in slots]
            if opening:
                refs.insert(0, (own.at[h, 1 - q_mod], 0.0))
            query = nq[h, q_mod]
            scores = [
                lax.dot_general(
                    ref[KEY], query, (((1,), (1,)), ((), ())), preferred_element_type=jnp.float32
                )
                for ref, _ in refs
            ]
            jobs.append((q_mod, refs, scores))
        tops = []
        for q_mod, refs, scores in jobs:
            top = None if opening else top_ref[h, q_mod]
            for score, (_, add) in zip(scores, refs):
                most = jnp.max(score, axis=0, keepdims=True) + add
                top = most if top is None else jnp.maximum(top, most)
            tops.append(top)
        results = []
        for (q_mod, refs, scores), top in zip(jobs, tops):
            total, mixed = None, None
            for score, (ref, add) in zip(scores, refs):
                weights = jnp.exp2((score - (top - add)) * FACTOR)
                part = jnp.sum(weights, axis=0, keepdims=True)
                value = jnp.concatenate(
                    [ref[VALUE, r : r + HEAD_DIM] for r in range(0, rows, HEAD_DIM)], axis=1
                )
                block = jnp.dot(
                    value, weights.astype(jnp.bfloat16), preferred_element_type=jnp.float32
                )
                total = part if total is None else total + part
                mixed = block if mixed is None else mixed + block
            if not opening:
                fade = jnp.exp2((top_ref[h, q_mod] - top) * FACTOR)
                total += total_ref[h, q_mod] * fade
                mixed += mixed_ref[h, q_mod] * fade
            results.append((q_mod, top, total, mixed))
        if closing:
            return [jnp.transpose(mixed / total).astype(jnp.bfloat16) for _, _, total, mixed in results]
        for q_mod, top, total, mixed in results:
            top_ref[h, q_mod] = top
            total_ref[h, q_mod] = total
            mixed_ref[h, q_mod] = mixed

    partner_copy(VALUE).wait_recv()
    partner_copy(KEY).wait_recv()

    def first_pass(h, carry):
        attend(h, (PARTNER,), opening=True)
        return carry

    lax.fori_loop(0, heads, first_pass, 0)

    start_relay(0)
    start_relay(1)
    finish_relay(0)

    def second_pass(h, carry):
        @pl.when(h + 1 < heads)
        def _():
            start_relay(h + 2)

        finish_relay(h + 1)

        @pl.when(behind)
        def _():
            direct_copy(h).wait_recv()

        cols = pl.ds(pl.multiple_of(h * HEAD_DIM, HEAD_DIM), HEAD_DIM)
        vout[:, cols], aout[:, cols] = attend(h, (NEAR, FAR, DIRECT), closing=True)
        return carry

    lax.fori_loop(0, heads, second_pass, 0)

    for by in range(1, count_head):
        sum_copy(by).wait_send()
    for kv in (KEY, VALUE):
        partner_copy(kv).wait_send()

    @pl.when(ahead)
    def _():
        for h in range(heads):
            direct_copy(h).wait_send()
        for part in range(heads + 1):
            relay_copy(NEAR, VIDEO, part).wait_send()

    @pl.when(behind)
    def _():
        for part in range(heads + 1):
            for slot, mod in SPLIT:
                split_copy(slot, mod, part).wait_send()
            relay_copy(FAR, AUDIO, part).wait_send()


def hand_over(v_in, a_in, v_out, a_out, held, sems_in, sems_out):
    parts = held.shape[1]
    rows = held.shape[2]
    refs = ((v_in, v_out), (a_in, a_out))
    taken, given = [], []
    for i, (src, dst) in enumerate(refs):
        for p in range(parts):
            cut = pl.ds(p * rows, rows)
            taken.append(pltpu.make_async_copy(src.at[cut], held.at[i, p], sems_in.at[i, p]))
            given.append(pltpu.make_async_copy(held.at[i, p], dst.at[cut], sems_out.at[i, p]))
    for copy in taken:
        copy.start()
    for before, after in zip(taken, given):
        before.wait()
        after.start()
    for copy in given:
        copy.wait()


def local(
    video_q,
    video_k,
    video_v,
    audio_q,
    audio_k,
    audio_v,
    video_q_gain,
    audio_k_gain,
    audio_q_gain,
    video_k_gain,
    tile_first,
    tile_count,
):
    count_seq, count_head = lax.axis_size("seq"), lax.axis_size("head")
    rows, cols = video_q.shape
    heads = cols // HEAD_DIM

    def body(*refs):
        kernel(count_seq, count_head, *refs)

    hbm = pl.BlockSpec(memory_space=pl.ANY)
    vmem = pl.BlockSpec(memory_space=pltpu.VMEM)
    smem = pl.BlockSpec(memory_space=pltpu.SMEM)
    both = (jax.ShapeDtypeStruct((rows, cols), jnp.bfloat16),) * 2
    dma = pltpu.SemaphoreType.DMA
    v_out, a_out = pl.pallas_call(
        body,
        out_shape=both,
        in_specs=[hbm] * 6 + [vmem] * 4 + [smem] * 2,
        out_specs=(vmem, vmem),
        scratch_shapes=[
            pltpu.VMEM((4, rows, cols), jnp.bfloat16),
            pltpu.VMEM((heads, 2, rows, HEAD_DIM), jnp.bfloat16),
            pltpu.VMEM((heads, 2, 2, rows, HEAD_DIM), jnp.bfloat16),
            pltpu.VMEM((heads, 2, rows, HEAD_DIM), jnp.bfloat16),
            pltpu.VMEM((4, heads, 2, 2, rows, HEAD_DIM), jnp.bfloat16),
            pltpu.VMEM((heads, 2, 1, rows), jnp.float32),
            pltpu.VMEM((heads, 2, 1, rows), jnp.float32),
            pltpu.VMEM((heads, 2, HEAD_DIM, rows), jnp.float32),
            pltpu.VMEM((8, rows), jnp.float32),
            pltpu.VMEM((count_head - 1, 8, rows), jnp.float32),
            dma((4,)),
            dma((2, heads)),
            dma((count_head - 1,)),
            dma((count_head - 1,)),
            dma((2,)),
            dma((2,)),
            dma((2, heads + 1)),
            dma((2, heads + 1)),
            dma((2, heads + 1)),
            dma((2, heads + 1)),
            dma((heads,)),
            dma((heads,)),
        ],
        compiler_params=pltpu.CompilerParams(
            collective_id=0, has_side_effects=True, vmem_limit_bytes=56 * 1024 * 1024
        ),
        name="attend",
    )(
        video_q,
        video_k,
        video_v,
        audio_q,
        audio_k,
        audio_v,
        video_q_gain,
        audio_k_gain,
        audio_q_gain,
        video_k_gain,
        tile_first,
        tile_count,
    )
    return pl.pallas_call(
        hand_over,
        out_shape=both,
        in_specs=[hbm] * 2,
        out_specs=(hbm, hbm),
        scratch_shapes=[
            pltpu.VMEM((2, 2, rows // 2, cols), jnp.bfloat16),
            dma((2, 2)),
            dma((2, 2)),
        ],
        compiler_params=pltpu.CompilerParams(vmem_limit_bytes=56 * 1024 * 1024),
        name="hand_over",
    )(v_out, a_out)


def solution(mesh):
    return jax.shard_map(
        local,
        mesh=mesh,
        in_specs=(P("seq", "head"),) * 6 + (P("head"),) * 4 + (P(), P()),
        out_specs=(P("seq", "head"), P("seq", "head")),
        check_vma=False,
    )
```

```python
import jax
import jax.numpy as jnp
from jax import lax
from jax.experimental import pallas as pl
from jax.experimental.pallas import tpu as pltpu
from jax.sharding import PartitionSpec as P

HEAD_DIM = 128
EPS = 1e-06
NEG = -1e30
MESH = pl.DeviceIdType.MESH
LOG2E = 1.4426950408889634
FACTOR = LOG2E * HEAD_DIM**-0.5

PARTNER, DIRECT, NEAR, FAR = 0, 1, 2, 3
OFFSET = (1, -2, -1, 2)
AUDIO, VIDEO = 0, 1
KEY, VALUE = 0, 1
SPLIT = ((NEAR, AUDIO), (FAR, VIDEO))
RELAY = ((FAR, AUDIO), (NEAR, VIDEO))


def kernel(
    count_seq,
    count_head,
    vq_hbm,
    vk_hbm,
    vv_hbm,
    aq_hbm,
    ak_hbm,
    av_hbm,
    vqg,
    akg,
    aqg,
    vkg,
    first_ref,
    count_ref,
    vout,
    aout,
    raw,
    raw_v,
    own,
    nq,
    far,
    top_ref,
    total_ref,
    mixed_ref,
    sums,
    sums_in,
    local_sem,
    value_sem,
    sum_send,
    sum_recv,
    partner_send,
    partner_recv,
    split_send,
    split_recv,
    relay_send,
    relay_recv,
    direct_send,
    direct_recv,
):
    seq = lax.axis_index("seq")
    head = lax.axis_index("head")
    sigma = 1 - 2 * lax.rem(seq, 2)
    heads = nq.shape[0]
    rows = raw.shape[1]
    width = raw.shape[2] * count_head
    behind = (seq - sigma >= 0) & (seq - sigma < count_seq)
    ahead = (seq + 2 * sigma >= 0) & (seq + 2 * sigma < count_seq)

    loads = []
    for i, ref in enumerate((ak_hbm, vk_hbm, vq_hbm, aq_hbm)):
        loads.append(pltpu.make_async_copy(ref, raw.at[i], local_sem.at[i]))
    value_loads = []
    for mod, ref in enumerate((av_hbm, vv_hbm)):
        for h in range(heads):
            value_loads.append(
                pltpu.make_async_copy(
                    ref.at[:, pl.ds(h * HEAD_DIM, HEAD_DIM)],
                    raw_v.at[h, mod],
                    value_sem.at[mod, h],
                )
            )
    barrier = pltpu.get_barrier_semaphore()

    def greet(by):
        pl.semaphore_signal(barrier, inc=1, device_id=(seq + by * sigma, head), device_id_type=MESH)

    greet(1)
    for by in range(1, count_head):
        pl.semaphore_signal(
            barrier, inc=1, device_id=(seq, lax.rem(head + by, count_head)), device_id_type=MESH
        )

    @pl.when(behind)
    def _():
        greet(-1)
        greet(-2)

    @pl.when(ahead)
    def _():
        greet(2)

    for load in value_loads + loads:
        load.start()
    for load in value_loads:
        load.wait()
    for h in range(heads):
        for mod in (AUDIO, VIDEO):
            for r in range(0, rows, HEAD_DIM):
                own[h, mod, VALUE, r : r + HEAD_DIM] = jnp.transpose(raw_v[h, mod, r : r + HEAD_DIM])
    peers = count_head + 2 * behind.astype(jnp.int32) + ahead.astype(jnp.int32)
    pl.semaphore_wait(barrier, peers)

    def remote(src, dst, send, recv, by):
        return pltpu.make_async_remote_copy(
            src_ref=src,
            dst_ref=dst,
            send_sem=send,
            recv_sem=recv,
            device_id=(seq + by * sigma, head),
            device_id_type=MESH,
        )

    def block(ref, mod, part):
        if isinstance(part, int) and part == 0:
            return ref.at[:, mod, VALUE]
        return ref.at[part - 1, mod, KEY]

    def split_copy(slot, mod, part):
        by = -1 if slot == NEAR else -2
        return remote(
            block(own, mod, part),
            block(far.at[slot], mod, part),
            split_send.at[mod, part],
            split_recv.at[mod, part],
            by,
        )

    def relay_copy(slot, mod, part):
        held = NEAR if slot == FAR else FAR
        return remote(
            block(far.at[held], mod, part),
            block(far.at[slot], mod, part),
            relay_send.at[mod, part],
            relay_recv.at[mod, part],
            1,
        )

    def partner_copy(kv):
        return remote(own.at[:, :, kv], far.at[PARTNER, :, :, kv], partner_send.at[kv], partner_recv.at[kv], 1)

    def direct_copy(h):
        return remote(own.at[h], far.at[DIRECT, h], direct_send.at[h], direct_recv.at[h], 2)

    def start_split(part):
        @pl.when(behind)
        def _():
            for slot, mod in SPLIT:
                split_copy(slot, mod, part).start()

    def start_relay(part):
        @pl.when(behind)
        def _():
            split_copy(NEAR, AUDIO, part).wait_recv()
            relay_copy(FAR, AUDIO, part).start()

        @pl.when(ahead)
        def _():
            split_copy(FAR, VIDEO, part).wait_recv()
            relay_copy(NEAR, VIDEO, part).start()

    def finish_relay(part):
        @pl.when(ahead)
        def _():
            relay_copy(FAR, AUDIO, part).wait_recv()

        @pl.when(behind)
        def _():
            relay_copy(NEAR, VIDEO, part).wait_recv()

    start_split(0)
    partner_copy(VALUE).start()

    def clear(slot):
        def body(h, carry):
            far[slot, h] = jnp.zeros(far.shape[2:], far.dtype)
            return carry

        lax.fori_loop(0, heads, body, 0)

    @pl.when(jnp.logical_not(behind))
    def _():
        clear(DIRECT)
        clear(NEAR)

    @pl.when(jnp.logical_not(ahead))
    def _():
        clear(FAR)

    lane = lax.broadcasted_iota(jnp.int32, (rows, HEAD_DIM), 1)
    packed = jnp.zeros((rows, HEAD_DIM), jnp.float32)
    for i in range(4):
        loads[i].wait()
        total = jnp.zeros((rows, HEAD_DIM), jnp.float32)
        for h in range(heads):
            wide = raw[i, :, h * HEAD_DIM : (h + 1) * HEAD_DIM].astype(jnp.float32)
            total += wide * wide
        packed = jnp.where(lane == i, jnp.sum(total, axis=1, keepdims=True), packed)
    sums[...] = jnp.transpose(packed)[:8]

    def sum_copy(by):
        return pltpu.make_async_remote_copy(
            src_ref=sums,
            dst_ref=sums_in.at[by - 1],
            send_sem=sum_send.at[by - 1],
            recv_sem=sum_recv.at[by - 1],
            device_id=(seq, lax.rem(head + by, count_head)),
            device_id_type=MESH,
        )

    for by in range(1, count_head):
        sum_copy(by).start()
    all_sums = sums[...]
    for by in range(1, count_head):
        sum_copy(by).wait_recv()
        all_sums += sums_in[by - 1]
    scale = lax.rsqrt(all_sums / width + EPS)
    scale = jnp.transpose(jnp.concatenate([scale] * (HEAD_DIM // 8), axis=0))

    def normalized(i, gain, h):
        cols = slice(h * HEAD_DIM, (h + 1) * HEAD_DIM)
        wide = raw[i, :, cols].astype(jnp.float32)
        return (wide * scale[:, i : i + 1] * gain[cols]).astype(jnp.bfloat16)

    for h in range(heads):
        own[h, AUDIO, KEY] = normalized(0, akg, h)
        own[h, VIDEO, KEY] = normalized(1, vkg, h)
        start_split(h + 1)

        @pl.when(ahead)
        def _():
            direct_copy(h).start()

    partner_copy(KEY).start()
    for h in range(heads):
        nq[h, VIDEO] = normalized(2, vqg, h)
        nq[h, AUDIO] = normalized(3, aqg, h)

    def covers(stretch, tile):
        safe = lax.rem(stretch + count_seq, count_seq)
        first = first_ref[safe]
        inside = (stretch >= 0) & (stretch < count_seq) & (tile >= 0) & (tile < count_seq)
        return inside & (tile >= first) & (tile < first + count_ref[safe])

    bias = ([], [])
    for slot in range(4):
        other = seq + OFFSET[slot] * sigma
        bias[VIDEO].append(jnp.where(covers(other, seq), 0.0, NEG))
        bias[AUDIO].append(jnp.where(covers(seq, other), 0.0, NEG))

    def attend(h, slots, opening=False, closing=False):
        jobs = []
        for q_mod in (VIDEO, AUDIO):
            refs = [(far.at[slot, h, 1 - q_mod], bias[q_mod][slot]) for slot in slots]
            if opening:
                refs.insert(0, (own.at[h, 1 - q_mod], 0.0))
            query = nq[h, q_mod]
            scores = [
                lax.dot_general(
                    ref[KEY], query, (((1,), (1,)), ((), ())), preferred_element_type=jnp.float32
                )
                for ref, _ in refs
            ]
            jobs.append((q_mod, refs, scores))
        tops = []
        for q_mod, refs, scores in jobs:
            top = None if opening else top_ref[h, q_mod]
            for score, (_, add) in zip(scores, refs):
                most = jnp.max(score, axis=0, keepdims=True) + add
                top = most if top is None else jnp.maximum(top, most)
            tops.append(top)
        results = []
        for (q_mod, refs, scores), top in zip(jobs, tops):
            total, mixed = None, None
            for score, (ref, add) in zip(scores, refs):
                weights = jnp.exp2((score - (top - add)) * FACTOR)
                part = jnp.sum(weights, axis=0, keepdims=True)
                value = jnp.concatenate(
                    [ref[VALUE, r : r + HEAD_DIM] for r in range(0, rows, HEAD_DIM)], axis=1
                )
                block = jnp.dot(
                    value, weights.astype(jnp.bfloat16), preferred_element_type=jnp.float32
                )
                total = part if total is None else total + part
                mixed = block if mixed is None else mixed + block
            if not opening:
                fade = jnp.exp2((top_ref[h, q_mod] - top) * FACTOR)
                total += total_ref[h, q_mod] * fade
                mixed += mixed_ref[h, q_mod] * fade
            results.append((q_mod, top, total, mixed))
        if closing:
            return [jnp.transpose(mixed / total).astype(jnp.bfloat16) for _, _, total, mixed in results]
        for q_mod, top, total, mixed in results:
            top_ref[h, q_mod] = top
            total_ref[h, q_mod] = total
            mixed_ref[h, q_mod] = mixed

    partner_copy(VALUE).wait_recv()
    partner_copy(KEY).wait_recv()

    def first_pass(h, carry):
        attend(h, (PARTNER,), opening=True)
        return carry

    lax.fori_loop(0, heads, first_pass, 0)

    start_relay(0)
    start_relay(1)
    finish_relay(0)

    def second_pass(h, carry):
        @pl.when(h + 1 < heads)
        def _():
            start_relay(h + 2)

        finish_relay(h + 1)
        attend(h, (NEAR, FAR))

        @pl.when(h >= 1)
        def _():
            last_pass(h - 1)

        return carry

    def last_pass(h):
        @pl.when(behind)
        def _():
            direct_copy(h).wait_recv()

        cols = pl.ds(pl.multiple_of(h * HEAD_DIM, HEAD_DIM), HEAD_DIM)
        vout[:, cols], aout[:, cols] = attend(h, (DIRECT,), closing=True)

    lax.fori_loop(0, heads, second_pass, 0)
    last_pass(heads - 1)

    for by in range(1, count_head):
        sum_copy(by).wait_send()
    for kv in (KEY, VALUE):
        partner_copy(kv).wait_send()

    @pl.when(ahead)
    def _():
        for h in range(heads):
            direct_copy(h).wait_send()
        for part in range(heads + 1):
            relay_copy(NEAR, VIDEO, part).wait_send()

    @pl.when(behind)
    def _():
        for part in range(heads + 1):
            for slot, mod in SPLIT:
                split_copy(slot, mod, part).wait_send()
            relay_copy(FAR, AUDIO, part).wait_send()


def hand_over(v_in, a_in, v_out, a_out, sems):
    parts = sems.shape[1]
    rows = v_in.shape[0] // parts
    copies = []
    for i, (src, dst) in enumerate(((v_in, v_out), (a_in, a_out))):
        for p in range(parts):
            cut = pl.ds(p * rows, rows)
            copies.append(pltpu.make_async_copy(src.at[cut], dst.at[cut], sems.at[i, p]))
    for copy in copies:
        copy.start()
    for copy in copies:
        copy.wait()


def local(
    video_q,
    video_k,
    video_v,
    audio_q,
    audio_k,
    audio_v,
    video_q_gain,
    audio_k_gain,
    audio_q_gain,
    video_k_gain,
    tile_first,
    tile_count,
):
    count_seq, count_head = lax.axis_size("seq"), lax.axis_size("head")
    rows, cols = video_q.shape
    heads = cols // HEAD_DIM

    def body(*refs):
        kernel(count_seq, count_head, *refs)

    hbm = pl.BlockSpec(memory_space=pl.ANY)
    vmem = pl.BlockSpec(memory_space=pltpu.VMEM)
    smem = pl.BlockSpec(memory_space=pltpu.SMEM)
    both = (jax.ShapeDtypeStruct((rows, cols), jnp.bfloat16),) * 2
    dma = pltpu.SemaphoreType.DMA
    v_out, a_out = pl.pallas_call(
        body,
        out_shape=(pltpu.VMEM((rows, cols), jnp.bfloat16),) * 2,
        in_specs=[hbm] * 6 + [vmem] * 4 + [smem] * 2,
        out_specs=(vmem, vmem),
        scratch_shapes=[
            pltpu.VMEM((4, rows, cols), jnp.bfloat16),
            pltpu.VMEM((heads, 2, rows, HEAD_DIM), jnp.bfloat16),
            pltpu.VMEM((heads, 2, 2, rows, HEAD_DIM), jnp.bfloat16),
            pltpu.VMEM((heads, 2, rows, HEAD_DIM), jnp.bfloat16),
            pltpu.VMEM((4, heads, 2, 2, rows, HEAD_DIM), jnp.bfloat16),
            pltpu.VMEM((heads, 2, 1, rows), jnp.float32),
            pltpu.VMEM((heads, 2, 1, rows), jnp.float32),
            pltpu.VMEM((heads, 2, HEAD_DIM, rows), jnp.float32),
            pltpu.VMEM((8, rows), jnp.float32),
            pltpu.VMEM((count_head - 1, 8, rows), jnp.float32),
            dma((4,)),
            dma((2, heads)),
            dma((count_head - 1,)),
            dma((count_head - 1,)),
            dma((2,)),
            dma((2,)),
            dma((2, heads + 1)),
            dma((2, heads + 1)),
            dma((2, heads + 1)),
            dma((2, heads + 1)),
            dma((heads,)),
            dma((heads,)),
        ],
        compiler_params=pltpu.CompilerParams(
            collective_id=0, has_side_effects=True, vmem_limit_bytes=40 * 1024 * 1024
        ),
        name="attend",
    )(
        *(
            pltpu.with_memory_space_constraint(x, pltpu.HBM)
            for x in (
                video_q,
                video_k,
                video_v,
                audio_q,
                audio_k,
                audio_v,
                video_q_gain,
                audio_k_gain,
                audio_q_gain,
                video_k_gain,
                tile_first,
                tile_count,
            )
        )
    )
    return pl.pallas_call(
        hand_over,
        out_shape=both,
        in_specs=[vmem] * 2,
        out_specs=(hbm, hbm),
        scratch_shapes=[dma((2, 2))],
        compiler_params=pltpu.CompilerParams(vmem_limit_bytes=4 * 1024 * 1024),
        name="hand_over",
    )(*(pltpu.with_memory_space_constraint(x, pltpu.VMEM) for x in (v_out, a_out)))


def solution(mesh):
    return jax.shard_map(
        local,
        mesh=mesh,
        in_specs=(P("seq", "head"),) * 6 + (P("head"),) * 4 + (P(), P()),
        out_specs=(P("seq", "head"), P("seq", "head")),
        check_vma=False,
    )
```

```python
import jax
import jax.numpy as jnp
from jax import lax
from jax.experimental import pallas as pl
from jax.experimental.pallas import tpu as pltpu
from jax.sharding import PartitionSpec as P

HEAD_DIM = 128
EPS = 1e-06
NEG = -1e30
EARLY = 2
MESH = pl.DeviceIdType.MESH
LOG2E = 1.4426950408889634
FACTOR = LOG2E * HEAD_DIM**-0.5

PARTNER, DIRECT, NEAR, FAR = 0, 1, 2, 3
OFFSET = (1, -2, -1, 2)
AUDIO, VIDEO = 0, 1
KEY, VALUE = 0, 1
SPLIT = ((NEAR, AUDIO), (FAR, VIDEO))
RELAY = ((FAR, AUDIO), (NEAR, VIDEO))


def kernel(
    count_seq,
    count_head,
    vq_hbm,
    vk_hbm,
    vv_hbm,
    aq_hbm,
    ak_hbm,
    av_hbm,
    vqg,
    akg,
    aqg,
    vkg,
    first_ref,
    count_ref,
    vout,
    aout,
    raw,
    raw_v,
    own,
    nq,
    far,
    top_ref,
    total_ref,
    mixed_ref,
    sums,
    sums_in,
    all_sums,
    local_sem,
    value_sem,
    pair_send,
    pair_recv,
    sum_send,
    sum_recv,
    partner_send,
    partner_recv,
    split_send,
    split_recv,
    relay_send,
    relay_recv,
    direct_send,
    direct_recv,
):
    seq = lax.axis_index("seq")
    head = lax.axis_index("head")
    sigma = 1 - 2 * lax.rem(seq, 2)
    heads = nq.shape[0]
    rows = raw.shape[1]
    width = raw.shape[2] * count_head
    behind = (seq - sigma >= 0) & (seq - sigma < count_seq)
    ahead = (seq + 2 * sigma >= 0) & (seq + 2 * sigma < count_seq)

    loads = []
    for i, ref in enumerate((ak_hbm, vk_hbm, vq_hbm, aq_hbm)):
        loads.append(pltpu.make_async_copy(ref, raw.at[i], local_sem.at[i]))
    value_loads = []
    for mod, ref in enumerate((av_hbm, vv_hbm)):
        for h in range(heads):
            value_loads.append(
                pltpu.make_async_copy(
                    ref.at[:, pl.ds(h * HEAD_DIM, HEAD_DIM)],
                    raw_v.at[h, mod],
                    value_sem.at[mod, h],
                )
            )
    barrier = pltpu.get_barrier_semaphore()

    def greet(by):
        pl.semaphore_signal(barrier, inc=1, device_id=(seq + by * sigma, head), device_id_type=MESH)

    greet(1)

    lead = sigma > 0

    @pl.when(lead)
    def _():
        for by in range(1, count_head):
            pl.semaphore_signal(
                barrier, inc=1, device_id=(seq, lax.rem(head + by, count_head)), device_id_type=MESH
            )

    @pl.when(behind)
    def _():
        greet(-1)
        greet(-2)

    @pl.when(ahead)
    def _():
        greet(2)

    for load in value_loads + loads:
        load.start()
    for load in value_loads:
        load.wait()
    for h in range(heads):
        for mod in (AUDIO, VIDEO):
            for r in range(0, rows, HEAD_DIM):
                own[h, mod, VALUE, r : r + HEAD_DIM] = jnp.transpose(raw_v[h, mod, r : r + HEAD_DIM])
    peers = 1 + 2 * behind.astype(jnp.int32) + ahead.astype(jnp.int32)
    peers += (count_head - 1) * lead.astype(jnp.int32)
    pl.semaphore_wait(barrier, peers)

    def remote(src, dst, send, recv, by):
        return pltpu.make_async_remote_copy(
            src_ref=src,
            dst_ref=dst,
            send_sem=send,
            recv_sem=recv,
            device_id=(seq + by * sigma, head),
            device_id_type=MESH,
        )

    def block(ref, mod, part):
        if isinstance(part, int) and part == 0:
            return ref.at[:, mod, VALUE]
        return ref.at[part - 1, mod, KEY]

    def split_copy(slot, mod, part):
        by = -1 if slot == NEAR else -2
        return remote(
            block(own, mod, part),
            block(far.at[slot], mod, part),
            split_send.at[mod, part],
            split_recv.at[mod, part],
            by,
        )

    def relay_copy(slot, mod, part):
        held = NEAR if slot == FAR else FAR
        return remote(
            block(far.at[held], mod, part),
            block(far.at[slot], mod, part),
            relay_send.at[mod, part],
            relay_recv.at[mod, part],
            1,
        )

    def partner_copy(kv):
        return remote(own.at[:, :, kv], far.at[PARTNER, :, :, kv], partner_send.at[kv], partner_recv.at[kv], 1)

    def direct_copy(part):
        def block(ref):
            if part == 0:
                return ref.at[pl.ds(0, EARLY), :, VALUE]
            if part == 1:
                return ref.at[pl.ds(0, EARLY), :, KEY]
            return ref.at[part - 2 + EARLY]

        return remote(
            block(own), block(far.at[DIRECT]), direct_send.at[part], direct_recv.at[part], 2
        )

    direct_parts = heads - EARLY + 2

    def start_split(part):
        @pl.when(behind)
        def _():
            for slot, mod in SPLIT:
                split_copy(slot, mod, part).start()

    def start_relay(part):
        @pl.when(behind)
        def _():
            split_copy(NEAR, AUDIO, part).wait_recv()
            relay_copy(FAR, AUDIO, part).start()

        @pl.when(ahead)
        def _():
            split_copy(FAR, VIDEO, part).wait_recv()
            relay_copy(NEAR, VIDEO, part).start()

    def finish_relay(part):
        @pl.when(ahead)
        def _():
            relay_copy(FAR, AUDIO, part).wait_recv()

        @pl.when(behind)
        def _():
            relay_copy(NEAR, VIDEO, part).wait_recv()

    start_split(0)

    @pl.when(ahead)
    def _():
        direct_copy(0).start()

    partner_copy(VALUE).start()

    def clear(slot):
        def body(h, carry):
            far[slot, h] = jnp.zeros(far.shape[2:], far.dtype)
            return carry

        lax.fori_loop(0, heads, body, 0)

    @pl.when(jnp.logical_not(behind))
    def _():
        clear(DIRECT)
        clear(NEAR)

    @pl.when(jnp.logical_not(ahead))
    def _():
        clear(FAR)

    lane = lax.broadcasted_iota(jnp.int32, (rows, HEAD_DIM), 1)
    packed = jnp.zeros((rows, HEAD_DIM), jnp.float32)
    for i in range(4):
        loads[i].wait()
        total = jnp.zeros((rows, HEAD_DIM), jnp.float32)
        for h in range(heads):
            wide = raw[i, :, h * HEAD_DIM : (h + 1) * HEAD_DIM].astype(jnp.float32)
            total += wide * wide
        packed = jnp.where(lane == i, jnp.sum(total, axis=1, keepdims=True), packed)
    core = lax.rem(seq, 2)
    sums[core] = jnp.transpose(packed)[:8]

    def sum_copy(by):
        return pltpu.make_async_remote_copy(
            src_ref=sums,
            dst_ref=sums_in.at[by - 1],
            send_sem=sum_send.at[by - 1],
            recv_sem=sum_recv.at[by - 1],
            device_id=(seq, lax.rem(head + by, count_head)),
            device_id_type=MESH,
        )

    up_copy = remote(sums.at[1], sums.at[1], pair_send.at[0], pair_recv.at[0], 1)
    back_copy = remote(all_sums.at[1], all_sums.at[1], pair_send.at[1], pair_recv.at[1], 1)

    @pl.when(lead)
    def _():
        up_copy.wait_recv()
        for by in range(1, count_head):
            sum_copy(by).start()
        total = sums[...]
        for by in range(1, count_head):
            sum_copy(by).wait_recv()
            total += sums_in[by - 1]
        all_sums[...] = total
        back_copy.start()

    @pl.when(jnp.logical_not(lead))
    def _():
        up_copy.start()
        back_copy.wait_recv()

    scale = lax.rsqrt(all_sums[core] / width + EPS)
    scale = jnp.transpose(jnp.concatenate([scale] * (HEAD_DIM // 8), axis=0))

    def normalized(i, gain, h):
        cols = slice(h * HEAD_DIM, (h + 1) * HEAD_DIM)
        wide = raw[i, :, cols].astype(jnp.float32)
        return (wide * scale[:, i : i + 1] * gain[cols]).astype(jnp.bfloat16)

    for h in range(heads):
        own[h, AUDIO, KEY] = normalized(0, akg, h)
        own[h, VIDEO, KEY] = normalized(1, vkg, h)
        start_split(h + 1)

    partner_copy(KEY).start()
    for h in range(heads):
        nq[h, VIDEO] = normalized(2, vqg, h)
        nq[h, AUDIO] = normalized(3, aqg, h)

    def covers(stretch, tile):
        safe = lax.rem(stretch + count_seq, count_seq)
        first = first_ref[safe]
        inside = (stretch >= 0) & (stretch < count_seq) & (tile >= 0) & (tile < count_seq)
        return inside & (tile >= first) & (tile < first + count_ref[safe])

    bias = ([], [])
    for slot in range(4):
        other = seq + OFFSET[slot] * sigma
        bias[VIDEO].append(jnp.where(covers(other, seq), 0.0, NEG))
        bias[AUDIO].append(jnp.where(covers(seq, other), 0.0, NEG))

    def attend(h, slots, opening=False, closing=False):
        jobs = []
        for q_mod in (VIDEO, AUDIO):
            refs = [(far.at[slot, h, 1 - q_mod], bias[q_mod][slot]) for slot in slots]
            if opening:
                refs.insert(0, (own.at[h, 1 - q_mod], 0.0))
            query = nq[h, q_mod]
            scores = [
                lax.dot_general(
                    ref[KEY], query, (((1,), (1,)), ((), ())), preferred_element_type=jnp.float32
                )
                for ref, _ in refs
            ]
            jobs.append((q_mod, refs, scores))
        tops = []
        for q_mod, refs, scores in jobs:
            top = None if opening else top_ref[h, q_mod]
            for score, (_, add) in zip(scores, refs):
                most = jnp.max(score, axis=0, keepdims=True) + add
                top = most if top is None else jnp.maximum(top, most)
            tops.append(top)
        results = []
        for (q_mod, refs, scores), top in zip(jobs, tops):
            total, mixed = None, None
            for score, (ref, add) in zip(scores, refs):
                weights = jnp.exp2((score - (top - add)) * FACTOR)
                part = jnp.sum(weights, axis=0, keepdims=True)
                value = jnp.concatenate(
                    [ref[VALUE, r : r + HEAD_DIM] for r in range(0, rows, HEAD_DIM)], axis=1
                )
                block = jnp.dot(
                    value, weights.astype(jnp.bfloat16), preferred_element_type=jnp.float32
                )
                total = part if total is None else total + part
                mixed = block if mixed is None else mixed + block
            if not opening:
                fade = jnp.exp2((top_ref[h, q_mod] - top) * FACTOR)
                total += total_ref[h, q_mod] * fade
                mixed += mixed_ref[h, q_mod] * fade
            results.append((q_mod, top, total, mixed))
        if closing:
            return [jnp.transpose(mixed / total).astype(jnp.bfloat16) for _, _, total, mixed in results]
        for q_mod, top, total, mixed in results:
            top_ref[h, q_mod] = top
            total_ref[h, q_mod] = total
            mixed_ref[h, q_mod] = mixed

    partner_copy(VALUE).wait_recv()
    partner_copy(KEY).wait_recv()

    def first_pass(h, carry):
        attend(h, (PARTNER,), opening=True)
        return carry

    lax.fori_loop(0, heads, first_pass, 0)
    @pl.when(ahead)
    def _():
        for part in range(1, direct_parts):
            direct_copy(part).start()


    start_relay(0)
    start_relay(1)
    finish_relay(0)

    def second_pass(h, carry):
        @pl.when(h + 1 < heads)
        def _():
            start_relay(h + 2)

        finish_relay(h + 1)
        attend(h, (NEAR, FAR))

        @pl.when(h >= 1)
        def _():
            last_pass(h - 1)

        return carry

    def last_pass(h):
        @pl.when(behind & (h == 0))
        def _():
            direct_copy(0).wait_recv()
            direct_copy(1).wait_recv()

        @pl.when(behind & (h >= EARLY))
        def _():
            arrived = h - EARLY + 2
            remote(
                own.at[h], far.at[DIRECT, h], direct_send.at[arrived], direct_recv.at[arrived], 2
            ).wait_recv()

        cols = pl.ds(pl.multiple_of(h * HEAD_DIM, HEAD_DIM), HEAD_DIM)
        vout[:, cols], aout[:, cols] = attend(h, (DIRECT,), closing=True)

    lax.fori_loop(0, heads, second_pass, 0)

    @pl.when(lead)
    def _():
        for by in range(1, count_head):
            sum_copy(by).wait_send()
        back_copy.wait_send()

    @pl.when(jnp.logical_not(lead))
    def _():
        up_copy.wait_send()

    for kv in (KEY, VALUE):
        partner_copy(kv).wait_send()

    @pl.when(behind)
    def _():
        for part in range(heads + 1):
            for slot, mod in SPLIT:
                split_copy(slot, mod, part).wait_send()
            relay_copy(FAR, AUDIO, part).wait_send()

    @pl.when(ahead)
    def _():
        for part in range(heads + 1):
            relay_copy(NEAR, VIDEO, part).wait_send()
        for part in range(direct_parts - 1):
            direct_copy(part).wait_send()

    last_pass(heads - 1)

    @pl.when(ahead)
    def _():
        direct_copy(direct_parts - 1).wait_send()


def hand_over(v_in, a_in, v_out, a_out, sems):
    parts = sems.shape[1]
    rows = v_in.shape[0] // parts
    copies = []
    for i, (src, dst) in enumerate(((v_in, v_out), (a_in, a_out))):
        for p in range(parts):
            cut = pl.ds(p * rows, rows)
            copies.append(pltpu.make_async_copy(src.at[cut], dst.at[cut], sems.at[i, p]))
    for copy in copies:
        copy.start()
    for copy in copies:
        copy.wait()


def local(
    video_q,
    video_k,
    video_v,
    audio_q,
    audio_k,
    audio_v,
    video_q_gain,
    audio_k_gain,
    audio_q_gain,
    video_k_gain,
    tile_first,
    tile_count,
):
    count_seq, count_head = lax.axis_size("seq"), lax.axis_size("head")
    rows, cols = video_q.shape
    heads = cols // HEAD_DIM

    def body(*refs):
        kernel(count_seq, count_head, *refs)

    hbm = pl.BlockSpec(memory_space=pl.ANY)
    vmem = pl.BlockSpec(memory_space=pltpu.VMEM)
    smem = pl.BlockSpec(memory_space=pltpu.SMEM)
    both = (jax.ShapeDtypeStruct((rows, cols), jnp.bfloat16),) * 2
    dma = pltpu.SemaphoreType.DMA
    v_out, a_out = pl.pallas_call(
        body,
        out_shape=(pltpu.VMEM((rows, cols), jnp.bfloat16),) * 2,
        in_specs=[hbm] * 6 + [vmem] * 4 + [smem] * 2,
        out_specs=(vmem, vmem),
        scratch_shapes=[
            pltpu.VMEM((4, rows, cols), jnp.bfloat16),
            pltpu.VMEM((heads, 2, rows, HEAD_DIM), jnp.bfloat16),
            pltpu.VMEM((heads, 2, 2, rows, HEAD_DIM), jnp.bfloat16),
            pltpu.VMEM((heads, 2, rows, HEAD_DIM), jnp.bfloat16),
            pltpu.VMEM((4, heads, 2, 2, rows, HEAD_DIM), jnp.bfloat16),
            pltpu.VMEM((heads, 2, 1, rows), jnp.float32),
            pltpu.VMEM((heads, 2, 1, rows), jnp.float32),
            pltpu.VMEM((heads, 2, HEAD_DIM, rows), jnp.float32),
            pltpu.VMEM((2, 8, rows), jnp.float32),
            pltpu.VMEM((count_head - 1, 2, 8, rows), jnp.float32),
            pltpu.VMEM((2, 8, rows), jnp.float32),
            dma((4,)),
            dma((2, heads)),
            dma((2,)),
            dma((2,)),
            dma((count_head - 1,)),
            dma((count_head - 1,)),
            dma((2,)),
            dma((2,)),
            dma((2, heads + 1)),
            dma((2, heads + 1)),
            dma((2, heads + 1)),
            dma((2, heads + 1)),
            dma((heads - EARLY + 2,)),
            dma((heads - EARLY + 2,)),
        ],
        compiler_params=pltpu.CompilerParams(
            collective_id=0, has_side_effects=True, vmem_limit_bytes=40 * 1024 * 1024
        ),
        name="attend",
    )(
        *(
            pltpu.with_memory_space_constraint(x, pltpu.HBM)
            for x in (
                video_q,
                video_k,
                video_v,
                audio_q,
                audio_k,
                audio_v,
                video_q_gain,
                audio_k_gain,
                audio_q_gain,
                video_k_gain,
                tile_first,
                tile_count,
            )
        )
    )
    return pl.pallas_call(
        hand_over,
        out_shape=both,
        in_specs=[vmem] * 2,
        out_specs=(hbm, hbm),
        scratch_shapes=[dma((2, 1))],
        compiler_params=pltpu.CompilerParams(vmem_limit_bytes=4 * 1024 * 1024),
        name="hand_over",
    )(*(pltpu.with_memory_space_constraint(x, pltpu.VMEM) for x in (v_out, a_out)))


def solution(mesh):
    return jax.shard_map(
        local,
        mesh=mesh,
        in_specs=(P("seq", "head"),) * 6 + (P("head"),) * 4 + (P(), P()),
        out_specs=(P("seq", "head"), P("seq", "head")),
        check_vma=False,
    )
```

```python
import jax
import jax.numpy as jnp
from jax import lax
from jax.experimental import pallas as pl
from jax.experimental.pallas import tpu as pltpu
from jax.sharding import PartitionSpec as P

HEAD_DIM = 128
EPS = 1e-06
NEG = -1e30
EARLY = 2
MESH = pl.DeviceIdType.MESH
LOG2E = 1.4426950408889634
FACTOR = LOG2E * HEAD_DIM**-0.5

PARTNER, DIRECT, NEAR, FAR = 0, 1, 2, 3
OFFSET = (1, -2, -1, 2)
AUDIO, VIDEO = 0, 1
KEY, VALUE = 0, 1
SPLIT = ((NEAR, AUDIO), (FAR, VIDEO))
RELAY = ((FAR, AUDIO), (NEAR, VIDEO))


def kernel(
    count_seq,
    count_head,
    vq_hbm,
    vk_hbm,
    vv_hbm,
    aq_hbm,
    ak_hbm,
    av_hbm,
    vqg_hbm,
    akg_hbm,
    aqg_hbm,
    vkg_hbm,
    first_hbm,
    count_hbm,
    vout,
    aout,
    vqg,
    akg,
    aqg,
    vkg,
    first_ref,
    count_ref,
    small_sem,
    raw,
    raw_v,
    own,
    nq,
    far,
    top_ref,
    total_ref,
    mixed_ref,
    sums,
    sums_in,
    all_sums,
    local_sem,
    value_sem,
    pair_send,
    pair_recv,
    sum_send,
    sum_recv,
    partner_send,
    partner_recv,
    split_send,
    split_recv,
    relay_send,
    relay_recv,
    direct_send,
    direct_recv,
):
    seq = lax.axis_index("seq")
    head = lax.axis_index("head")
    sigma = 1 - 2 * lax.rem(seq, 2)
    heads = nq.shape[0]
    rows = raw.shape[1]
    width = raw.shape[2] * count_head
    behind = (seq - sigma >= 0) & (seq - sigma < count_seq)
    ahead = (seq + 2 * sigma >= 0) & (seq + 2 * sigma < count_seq)

    loads = []
    for i, ref in enumerate((ak_hbm, vk_hbm, vq_hbm, aq_hbm)):
        loads.append(pltpu.make_async_copy(ref, raw.at[i], local_sem.at[i]))
    value_loads = []
    for mod, ref in enumerate((av_hbm, vv_hbm)):
        for h in range(heads):
            value_loads.append(
                pltpu.make_async_copy(
                    ref.at[:, pl.ds(h * HEAD_DIM, HEAD_DIM)],
                    raw_v.at[h, mod],
                    value_sem.at[mod, h],
                )
            )
    smalls = [
        pltpu.make_async_copy(src, dst, small_sem.at[i])
        for i, (src, dst) in enumerate(
            (
                (akg_hbm, akg),
                (vkg_hbm, vkg),
                (vqg_hbm, vqg),
                (aqg_hbm, aqg),
                (first_hbm, first_ref),
                (count_hbm, count_ref),
            )
        )
    ]
    barrier = pltpu.get_barrier_semaphore()

    def greet(by):
        pl.semaphore_signal(barrier, inc=1, device_id=(seq + by * sigma, head), device_id_type=MESH)

    @pl.when(behind)
    def _():
        greet(-1)
        greet(-2)

    @pl.when(ahead)
    def _():
        greet(2)

    greet(1)

    lead = sigma > 0

    @pl.when(lead)
    def _():
        for by in range(1, count_head):
            pl.semaphore_signal(
                barrier, inc=1, device_id=(seq, lax.rem(head + by, count_head)), device_id_type=MESH
            )

    for load in value_loads + loads + smalls:
        load.start()
    for load in value_loads:
        load.wait()
    for h in range(heads):
        for mod in (AUDIO, VIDEO):
            for r in range(0, rows, HEAD_DIM):
                own[h, mod, VALUE, r : r + HEAD_DIM] = jnp.transpose(raw_v[h, mod, r : r + HEAD_DIM])
    peers = 1 + 2 * behind.astype(jnp.int32) + ahead.astype(jnp.int32)
    peers += (count_head - 1) * lead.astype(jnp.int32)
    pl.semaphore_wait(barrier, peers)

    def remote(src, dst, send, recv, by):
        return pltpu.make_async_remote_copy(
            src_ref=src,
            dst_ref=dst,
            send_sem=send,
            recv_sem=recv,
            device_id=(seq + by * sigma, head),
            device_id_type=MESH,
        )

    def block(ref, mod, part):
        if isinstance(part, int) and part == 0:
            return ref.at[:, mod, VALUE]
        return ref.at[part - 1, mod, KEY]

    def split_copy(slot, mod, part):
        by = -1 if slot == NEAR else -2
        return remote(
            block(own, mod, part),
            block(far.at[slot], mod, part),
            split_send.at[mod, part],
            split_recv.at[mod, part],
            by,
        )

    def relay_copy(slot, mod, part):
        held = NEAR if slot == FAR else FAR
        return remote(
            block(far.at[held], mod, part),
            block(far.at[slot], mod, part),
            relay_send.at[mod, part],
            relay_recv.at[mod, part],
            1,
        )

    def partner_copy(kv):
        return remote(own.at[:, :, kv], far.at[PARTNER, :, :, kv], partner_send.at[kv], partner_recv.at[kv], 1)

    def direct_copy(part):
        def block(ref):
            if part == 0:
                return ref.at[pl.ds(0, EARLY), :, VALUE]
            if part == 1:
                return ref.at[pl.ds(0, EARLY), :, KEY]
            if part == direct_parts - 3:
                return ref.at[heads - 1, :, KEY]
            if part >= direct_parts - 2:
                return ref.at[heads - 1, part - direct_parts + 2, VALUE]
            return ref.at[part - 2 + EARLY]

        return remote(
            block(own), block(far.at[DIRECT]), direct_send.at[part], direct_recv.at[part], 2
        )

    direct_parts = heads - EARLY + 4

    def start_split(part):
        @pl.when(behind)
        def _():
            for slot, mod in SPLIT:
                split_copy(slot, mod, part).start()

    def start_relay(part):
        @pl.when(behind)
        def _():
            split_copy(NEAR, AUDIO, part).wait_recv()
            relay_copy(FAR, AUDIO, part).start()

        @pl.when(ahead)
        def _():
            split_copy(FAR, VIDEO, part).wait_recv()
            relay_copy(NEAR, VIDEO, part).start()

    def finish_relay(part):
        @pl.when(ahead)
        def _():
            relay_copy(FAR, AUDIO, part).wait_recv()

        @pl.when(behind)
        def _():
            relay_copy(NEAR, VIDEO, part).wait_recv()

    start_split(0)

    @pl.when(ahead)
    def _():
        direct_copy(0).start()

    partner_copy(VALUE).start()

    def clear(slot):
        def body(h, carry):
            far[slot, h] = jnp.zeros(far.shape[2:], far.dtype)
            return carry

        lax.fori_loop(0, heads, body, 0)

    @pl.when(jnp.logical_not(behind))
    def _():
        clear(DIRECT)
        clear(NEAR)

    @pl.when(jnp.logical_not(ahead))
    def _():
        clear(FAR)

    lane = lax.broadcasted_iota(jnp.int32, (rows, HEAD_DIM), 1)
    packed = jnp.zeros((rows, HEAD_DIM), jnp.float32)
    for i in range(4):
        loads[i].wait()
        total = jnp.zeros((rows, HEAD_DIM), jnp.float32)
        for h in range(heads):
            wide = raw[i, :, h * HEAD_DIM : (h + 1) * HEAD_DIM].astype(jnp.float32)
            total += wide * wide
        packed = jnp.where(lane == i, jnp.sum(total, axis=1, keepdims=True), packed)
    for load in smalls:
        load.wait()
    core = lax.rem(seq, 2)
    sums[core] = jnp.transpose(packed)[:8]

    def sum_copy(by):
        return pltpu.make_async_remote_copy(
            src_ref=sums,
            dst_ref=sums_in.at[by - 1],
            send_sem=sum_send.at[by - 1],
            recv_sem=sum_recv.at[by - 1],
            device_id=(seq, lax.rem(head + by, count_head)),
            device_id_type=MESH,
        )

    up_copy = remote(sums.at[1], sums.at[1], pair_send.at[0], pair_recv.at[0], 1)
    back_copy = remote(all_sums.at[1], all_sums.at[1], pair_send.at[1], pair_recv.at[1], 1)

    @pl.when(lead)
    def _():
        up_copy.wait_recv()
        for by in range(1, count_head):
            sum_copy(by).start()
        total = sums[...]
        for by in range(1, count_head):
            sum_copy(by).wait_recv()
            total += sums_in[by - 1]
        all_sums[...] = total
        back_copy.start()

    @pl.when(jnp.logical_not(lead))
    def _():
        up_copy.start()
        back_copy.wait_recv()

    scale = lax.rsqrt(all_sums[core] / width + EPS)
    scale = jnp.transpose(jnp.concatenate([scale] * (HEAD_DIM // 8), axis=0))

    def normalized(i, gain, h):
        cols = slice(h * HEAD_DIM, (h + 1) * HEAD_DIM)
        wide = raw[i, :, cols].astype(jnp.float32)
        return (wide * scale[:, i : i + 1] * gain[cols]).astype(jnp.bfloat16)

    for h in range(heads):
        own[h, AUDIO, KEY] = normalized(0, akg, h)
        own[h, VIDEO, KEY] = normalized(1, vkg, h)
        start_split(h + 1)

    partner_copy(KEY).start()
    for h in range(heads):
        nq[h, VIDEO] = normalized(2, vqg, h)
        nq[h, AUDIO] = normalized(3, aqg, h)

    def covers(stretch, tile):
        safe = lax.rem(stretch + count_seq, count_seq)
        first = first_ref[safe]
        inside = (stretch >= 0) & (stretch < count_seq) & (tile >= 0) & (tile < count_seq)
        return inside & (tile >= first) & (tile < first + count_ref[safe])

    bias = ([], [])
    for slot in range(4):
        other = seq + OFFSET[slot] * sigma
        bias[VIDEO].append(jnp.where(covers(other, seq), 0.0, NEG))
        bias[AUDIO].append(jnp.where(covers(seq, other), 0.0, NEG))

    def attend(h, slots, opening=False, closing=False, ready=None):
        jobs = []
        for q_mod in (VIDEO, AUDIO):
            refs = [(far.at[slot, h, 1 - q_mod], bias[q_mod][slot]) for slot in slots]
            if opening:
                refs.insert(0, (own.at[h, 1 - q_mod], 0.0))
            query = nq[h, q_mod]
            scores = [
                lax.dot_general(
                    ref[KEY], query, (((1,), (1,)), ((), ())), preferred_element_type=jnp.float32
                )
                for ref, _ in refs
            ]
            jobs.append((q_mod, refs, scores))
        tops = []
        for q_mod, refs, scores in jobs:
            top = None if opening else top_ref[h, q_mod]
            for score, (_, add) in zip(scores, refs):
                most = jnp.max(score, axis=0, keepdims=True) + add
                top = most if top is None else jnp.maximum(top, most)
            tops.append(top)
        parts = []
        for (q_mod, refs, scores), top in zip(jobs, tops):
            total, weights = None, []
            for score, (_, add) in zip(scores, refs):
                weight = jnp.exp2((score - (top - add)) * FACTOR)
                part = jnp.sum(weight, axis=0, keepdims=True)
                total = part if total is None else total + part
                weights.append(weight.astype(jnp.bfloat16))
            fade = None
            if not opening:
                fade = jnp.exp2((top_ref[h, q_mod] - top) * FACTOR)
                total += total_ref[h, q_mod] * fade
            parts.append((q_mod, refs, top, total, weights, fade))
        for q_mod, refs, top, total, weights, fade in parts:
            if ready is not None:
                ready(1 - q_mod)
            mixed = None if opening else mixed_ref[h, q_mod] * fade
            for weight, (ref, _) in zip(weights, refs):
                value = jnp.concatenate(
                    [ref[VALUE, r : r + HEAD_DIM] for r in range(0, rows, HEAD_DIM)], axis=1
                )
                block = jnp.dot(value, weight, preferred_element_type=jnp.float32)
                mixed = block if mixed is None else mixed + block
            if closing:
                cols = pl.ds(pl.multiple_of(h * HEAD_DIM, HEAD_DIM), HEAD_DIM)
                out = vout if q_mod == VIDEO else aout
                out[:, cols] = jnp.transpose(mixed / total).astype(jnp.bfloat16)
            else:
                top_ref[h, q_mod] = top
                total_ref[h, q_mod] = total
                mixed_ref[h, q_mod] = mixed

    partner_copy(VALUE).wait_recv()
    partner_copy(KEY).wait_recv()

    def first_pass(h, carry):
        attend(h, (PARTNER,), opening=True)
        return carry

    lax.fori_loop(0, heads, first_pass, 0)
    @pl.when(ahead)
    def _():
        for part in range(1, direct_parts):
            direct_copy(part).start()


    start_relay(0)
    start_relay(1)
    finish_relay(0)

    def second_pass(h, carry):
        @pl.when(h + 1 < heads)
        def _():
            start_relay(h + 2)

        finish_relay(h + 1)
        attend(h, (NEAR, FAR))

        @pl.when(h >= 1)
        def _():
            last_pass(h - 1)

        return carry

    def last_pass(h):
        @pl.when(behind & (h == 0))
        def _():
            direct_copy(0).wait_recv()
            direct_copy(1).wait_recv()

        @pl.when(behind & (h >= EARLY))
        def _():
            arrived = h - EARLY + 2
            remote(
                own.at[h], far.at[DIRECT, h], direct_send.at[arrived], direct_recv.at[arrived], 2
            ).wait_recv()

        attend(h, (DIRECT,), closing=True)

    def arrive(part):
        @pl.when(behind)
        def _():
            direct_copy(part).wait_recv()

    lax.fori_loop(0, heads, second_pass, 0)

    @pl.when(lead)
    def _():
        for by in range(1, count_head):
            sum_copy(by).wait_send()
        back_copy.wait_send()

    @pl.when(jnp.logical_not(lead))
    def _():
        up_copy.wait_send()

    for kv in (KEY, VALUE):
        partner_copy(kv).wait_send()

    @pl.when(behind)
    def _():
        for part in range(heads + 1):
            for slot, mod in SPLIT:
                split_copy(slot, mod, part).wait_send()
            relay_copy(FAR, AUDIO, part).wait_send()

    @pl.when(ahead)
    def _():
        for part in range(heads + 1):
            relay_copy(NEAR, VIDEO, part).wait_send()
        for part in range(direct_parts - 1):
            direct_copy(part).wait_send()

    arrive(direct_parts - 3)
    attend(
        heads - 1,
        (DIRECT,),
        closing=True,
        ready=lambda mod: arrive(direct_parts - 2 + mod),
    )

    @pl.when(ahead)
    def _():
        direct_copy(direct_parts - 1).wait_send()


def hand_over(v_in, a_in, v_out, a_out, sems):
    parts = sems.shape[1]
    rows = v_in.shape[0] // parts
    copies = []
    for i, (src, dst) in enumerate(((v_in, v_out), (a_in, a_out))):
        for p in range(parts):
            cut = pl.ds(p * rows, rows)
            copies.append(pltpu.make_async_copy(src.at[cut], dst.at[cut], sems.at[i, p]))
    for copy in copies:
        copy.start()
    for copy in copies:
        copy.wait()


def local(
    video_q,
    video_k,
    video_v,
    audio_q,
    audio_k,
    audio_v,
    video_q_gain,
    audio_k_gain,
    audio_q_gain,
    video_k_gain,
    tile_first,
    tile_count,
):
    count_seq, count_head = lax.axis_size("seq"), lax.axis_size("head")
    rows, cols = video_q.shape
    heads = cols // HEAD_DIM

    def body(*refs):
        kernel(count_seq, count_head, *refs)

    hbm = pl.BlockSpec(memory_space=pl.ANY)
    vmem = pl.BlockSpec(memory_space=pltpu.VMEM)
    both = (jax.ShapeDtypeStruct((rows, cols), jnp.bfloat16),) * 2
    dma = pltpu.SemaphoreType.DMA
    v_out, a_out = pl.pallas_call(
        body,
        out_shape=(pltpu.VMEM((rows, cols), jnp.bfloat16),) * 2,
        in_specs=[hbm] * 12,
        out_specs=(vmem, vmem),
        scratch_shapes=[
            *[pltpu.VMEM((cols,), jnp.float32)] * 4,
            *[pltpu.SMEM((count_seq,), jnp.int32)] * 2,
            dma((6,)),
            pltpu.VMEM((4, rows, cols), jnp.bfloat16),
            pltpu.VMEM((heads, 2, rows, HEAD_DIM), jnp.bfloat16),
            pltpu.VMEM((heads, 2, 2, rows, HEAD_DIM), jnp.bfloat16),
            pltpu.VMEM((heads, 2, rows, HEAD_DIM), jnp.bfloat16),
            pltpu.VMEM((4, heads, 2, 2, rows, HEAD_DIM), jnp.bfloat16),
            pltpu.VMEM((heads, 2, 1, rows), jnp.float32),
            pltpu.VMEM((heads, 2, 1, rows), jnp.float32),
            pltpu.VMEM((heads, 2, HEAD_DIM, rows), jnp.float32),
            pltpu.VMEM((2, 8, rows), jnp.float32),
            pltpu.VMEM((count_head - 1, 2, 8, rows), jnp.float32),
            pltpu.VMEM((2, 8, rows), jnp.float32),
            dma((4,)),
            dma((2, heads)),
            dma((2,)),
            dma((2,)),
            dma((count_head - 1,)),
            dma((count_head - 1,)),
            dma((2,)),
            dma((2,)),
            dma((2, heads + 1)),
            dma((2, heads + 1)),
            dma((2, heads + 1)),
            dma((2, heads + 1)),
            dma((heads - EARLY + 4,)),
            dma((heads - EARLY + 4,)),
        ],
        compiler_params=pltpu.CompilerParams(
            collective_id=0, has_side_effects=True, vmem_limit_bytes=40 * 1024 * 1024
        ),
        name="attend",
    )(
        *(
            pltpu.with_memory_space_constraint(x, pltpu.HBM)
            for x in (
                video_q,
                video_k,
                video_v,
                audio_q,
                audio_k,
                audio_v,
                video_q_gain,
                audio_k_gain,
                audio_q_gain,
                video_k_gain,
                tile_first,
                tile_count,
            )
        )
    )
    return pl.pallas_call(
        hand_over,
        out_shape=both,
        in_specs=[vmem] * 2,
        out_specs=(hbm, hbm),
        scratch_shapes=[dma((2, 1))],
        compiler_params=pltpu.CompilerParams(vmem_limit_bytes=4 * 1024 * 1024),
        name="hand_over",
    )(*(pltpu.with_memory_space_constraint(x, pltpu.VMEM) for x in (v_out, a_out)))


def solution(mesh):
    return jax.shard_map(
        local,
        mesh=mesh,
        in_specs=(P("seq", "head"),) * 6 + (P("head"),) * 4 + (P(), P()),
        out_specs=(P("seq", "head"), P("seq", "head")),
        check_vma=False,
    )
```

```python
import jax
import jax.numpy as jnp
from jax import lax
from jax.experimental import pallas as pl
from jax.experimental.pallas import tpu as pltpu
from jax.sharding import PartitionSpec as P

HEAD_DIM = 128
EPS = 1e-06
NEG = -1e30
EARLY = 2
MESH = pl.DeviceIdType.MESH
LOG2E = 1.4426950408889634
FACTOR = LOG2E * HEAD_DIM**-0.5

PARTNER, DIRECT, NEAR, FAR = 0, 1, 2, 3
OFFSET = (1, -2, -1, 2)
AUDIO, VIDEO = 0, 1
KEY, VALUE = 0, 1
SPLIT = ((NEAR, AUDIO), (FAR, VIDEO))
RELAY = ((FAR, AUDIO), (NEAR, VIDEO))


def kernel(
    count_seq,
    count_head,
    vq_hbm,
    vk_hbm,
    vv_hbm,
    aq_hbm,
    ak_hbm,
    av_hbm,
    vqg_hbm,
    akg_hbm,
    aqg_hbm,
    vkg_hbm,
    first_hbm,
    count_hbm,
    vout,
    aout,
    vqg,
    akg,
    aqg,
    vkg,
    first_ref,
    count_ref,
    small_sem,
    raw,
    raw_v,
    own,
    nq,
    far,
    top_ref,
    total_ref,
    mixed_ref,
    sums,
    sums_in,
    all_sums,
    local_sem,
    value_sem,
    pair_send,
    pair_recv,
    sum_send,
    sum_recv,
    partner_send,
    partner_recv,
    split_send,
    split_recv,
    relay_send,
    relay_recv,
    direct_send,
    direct_recv,
):
    seq = lax.axis_index("seq")
    head = lax.axis_index("head")
    sigma = 1 - 2 * lax.rem(seq, 2)
    heads = nq.shape[0]
    rows = raw.shape[1]
    width = raw.shape[2] * count_head
    behind = (seq - sigma >= 0) & (seq - sigma < count_seq)
    ahead = (seq + 2 * sigma >= 0) & (seq + 2 * sigma < count_seq)

    loads = []
    for i, ref in enumerate((ak_hbm, vk_hbm, vq_hbm, aq_hbm)):
        loads.append(pltpu.make_async_copy(ref, raw.at[i], local_sem.at[i]))
    value_loads = [
        pltpu.make_async_copy(ref, raw_v.at[mod], value_sem.at[mod])
        for mod, ref in enumerate((av_hbm, vv_hbm))
    ]
    smalls = [
        pltpu.make_async_copy(src, dst, small_sem.at[i])
        for i, (src, dst) in enumerate(
            (
                (akg_hbm, akg),
                (vkg_hbm, vkg),
                (vqg_hbm, vqg),
                (aqg_hbm, aqg),
                (first_hbm, first_ref),
                (count_hbm, count_ref),
            )
        )
    ]
    barrier = pltpu.get_barrier_semaphore()

    def greet(by):
        pl.semaphore_signal(barrier, inc=1, device_id=(seq + by * sigma, head), device_id_type=MESH)

    @pl.when(behind)
    def _():
        greet(-1)
        greet(-2)

    @pl.when(ahead)
    def _():
        greet(2)

    greet(1)

    lead = sigma > 0

    @pl.when(lead)
    def _():
        for by in range(1, count_head):
            pl.semaphore_signal(
                barrier, inc=1, device_id=(seq, lax.rem(head + by, count_head)), device_id_type=MESH
            )

    for load in value_loads:
        load.start()
    for load in value_loads:
        load.wait()
    for h in range(heads):
        for mod in (AUDIO, VIDEO):
            for r in range(0, rows, HEAD_DIM):
                own[h, mod, VALUE, r : r + HEAD_DIM] = jnp.transpose(
                    raw_v[mod, r : r + HEAD_DIM, h * HEAD_DIM : (h + 1) * HEAD_DIM]
                )
    peers = 1 + 2 * behind.astype(jnp.int32) + ahead.astype(jnp.int32)
    peers += (count_head - 1) * lead.astype(jnp.int32)
    pl.semaphore_wait(barrier, peers)

    def remote(src, dst, send, recv, by):
        return pltpu.make_async_remote_copy(
            src_ref=src,
            dst_ref=dst,
            send_sem=send,
            recv_sem=recv,
            device_id=(seq + by * sigma, head),
            device_id_type=MESH,
        )

    def block(ref, mod, part):
        if isinstance(part, int) and part == 0:
            return ref.at[:, mod, VALUE]
        return ref.at[part - 1, mod, KEY]

    def split_copy(slot, mod, part):
        by = -1 if slot == NEAR else -2
        return remote(
            block(own, mod, part),
            block(far.at[slot], mod, part),
            split_send.at[mod, part],
            split_recv.at[mod, part],
            by,
        )

    def relay_copy(slot, mod, part):
        held = NEAR if slot == FAR else FAR
        return remote(
            block(far.at[held], mod, part),
            block(far.at[slot], mod, part),
            relay_send.at[mod, part],
            relay_recv.at[mod, part],
            1,
        )

    def partner_copy(kv):
        return remote(own.at[:, :, kv], far.at[PARTNER, :, :, kv], partner_send.at[kv], partner_recv.at[kv], 1)

    def direct_copy(part):
        def block(ref):
            if part == 0:
                return ref.at[pl.ds(0, EARLY), :, VALUE]
            if part == 1:
                return ref.at[pl.ds(0, EARLY), :, KEY]
            if part == direct_parts - 3:
                return ref.at[heads - 1, :, KEY]
            if part >= direct_parts - 2:
                return ref.at[heads - 1, part - direct_parts + 2, VALUE]
            return ref.at[part - 2 + EARLY]

        return remote(
            block(own), block(far.at[DIRECT]), direct_send.at[part], direct_recv.at[part], 2
        )

    direct_parts = heads - EARLY + 4

    def start_split(part):
        @pl.when(behind)
        def _():
            for slot, mod in SPLIT:
                split_copy(slot, mod, part).start()

    def start_relay(part):
        @pl.when(behind)
        def _():
            split_copy(NEAR, AUDIO, part).wait_recv()
            relay_copy(FAR, AUDIO, part).start()

        @pl.when(ahead)
        def _():
            split_copy(FAR, VIDEO, part).wait_recv()
            relay_copy(NEAR, VIDEO, part).start()

    def finish_relay(part):
        @pl.when(ahead)
        def _():
            relay_copy(FAR, AUDIO, part).wait_recv()

        @pl.when(behind)
        def _():
            relay_copy(NEAR, VIDEO, part).wait_recv()

    start_split(0)

    @pl.when(ahead)
    def _():
        direct_copy(0).start()

    partner_copy(VALUE).start()
    for load in loads + smalls:
        load.start()

    def clear(slot):
        def body(h, carry):
            far[slot, h] = jnp.zeros(far.shape[2:], far.dtype)
            return carry

        lax.fori_loop(0, heads, body, 0)

    @pl.when(jnp.logical_not(behind))
    def _():
        clear(DIRECT)
        clear(NEAR)

    @pl.when(jnp.logical_not(ahead))
    def _():
        clear(FAR)

    lane = lax.broadcasted_iota(jnp.int32, (rows, HEAD_DIM), 1)
    packed = jnp.zeros((rows, HEAD_DIM), jnp.float32)
    for i in range(4):
        loads[i].wait()
        total = jnp.zeros((rows, HEAD_DIM), jnp.float32)
        for h in range(heads):
            wide = raw[i, :, h * HEAD_DIM : (h + 1) * HEAD_DIM].astype(jnp.float32)
            total += wide * wide
        packed = jnp.where(lane == i, jnp.sum(total, axis=1, keepdims=True), packed)
    for load in smalls:
        load.wait()
    core = lax.rem(seq, 2)
    sums[core] = jnp.transpose(packed)[:8]

    def sum_copy(by):
        return pltpu.make_async_remote_copy(
            src_ref=sums,
            dst_ref=sums_in.at[by - 1],
            send_sem=sum_send.at[by - 1],
            recv_sem=sum_recv.at[by - 1],
            device_id=(seq, lax.rem(head + by, count_head)),
            device_id_type=MESH,
        )

    up_copy = remote(sums.at[1], sums.at[1], pair_send.at[0], pair_recv.at[0], 1)
    back_copy = remote(all_sums.at[1], all_sums.at[1], pair_send.at[1], pair_recv.at[1], 1)

    @pl.when(lead)
    def _():
        up_copy.wait_recv()
        for by in range(1, count_head):
            sum_copy(by).start()
        total = sums[...]
        for by in range(1, count_head):
            sum_copy(by).wait_recv()
            total += sums_in[by - 1]
        all_sums[...] = total
        back_copy.start()

    @pl.when(jnp.logical_not(lead))
    def _():
        up_copy.start()
        back_copy.wait_recv()

    scale = lax.rsqrt(all_sums[core] / width + EPS)
    scale = jnp.transpose(jnp.concatenate([scale] * (HEAD_DIM // 8), axis=0))

    def normalized(i, gain, h):
        cols = slice(h * HEAD_DIM, (h + 1) * HEAD_DIM)
        wide = raw[i, :, cols].astype(jnp.float32)
        return (wide * scale[:, i : i + 1] * gain[cols]).astype(jnp.bfloat16)

    for h in range(heads):
        own[h, AUDIO, KEY] = normalized(0, akg, h)
        own[h, VIDEO, KEY] = normalized(1, vkg, h)
        start_split(h + 1)

    partner_copy(KEY).start()
    for h in range(heads):
        nq[h, VIDEO] = normalized(2, vqg, h)
        nq[h, AUDIO] = normalized(3, aqg, h)

    def covers(stretch, tile):
        safe = lax.rem(stretch + count_seq, count_seq)
        first = first_ref[safe]
        inside = (stretch >= 0) & (stretch < count_seq) & (tile >= 0) & (tile < count_seq)
        return inside & (tile >= first) & (tile < first + count_ref[safe])

    bias = ([], [])
    for slot in range(4):
        other = seq + OFFSET[slot] * sigma
        bias[VIDEO].append(jnp.where(covers(other, seq), 0.0, NEG))
        bias[AUDIO].append(jnp.where(covers(seq, other), 0.0, NEG))

    def attend(h, slots, opening=False, closing=False, ready=None):
        jobs = []
        for q_mod in (VIDEO, AUDIO):
            refs = [(far.at[slot, h, 1 - q_mod], bias[q_mod][slot]) for slot in slots]
            if opening:
                refs.insert(0, (own.at[h, 1 - q_mod], 0.0))
            query = nq[h, q_mod]
            scores = [
                lax.dot_general(
                    ref[KEY], query, (((1,), (1,)), ((), ())), preferred_element_type=jnp.float32
                )
                for ref, _ in refs
            ]
            jobs.append((q_mod, refs, scores))
        tops = []
        for q_mod, refs, scores in jobs:
            top = None if opening else top_ref[h, q_mod]
            for score, (_, add) in zip(scores, refs):
                most = jnp.max(score, axis=0, keepdims=True) + add
                top = most if top is None else jnp.maximum(top, most)
            tops.append(top)
        parts = []
        for (q_mod, refs, scores), top in zip(jobs, tops):
            total, weights = None, []
            for score, (_, add) in zip(scores, refs):
                weight = jnp.exp2((score - (top - add)) * FACTOR)
                part = jnp.sum(weight, axis=0, keepdims=True)
                total = part if total is None else total + part
                weights.append(weight.astype(jnp.bfloat16))
            fade = None
            if not opening:
                fade = jnp.exp2((top_ref[h, q_mod] - top) * FACTOR)
                total += total_ref[h, q_mod] * fade
            parts.append((q_mod, refs, top, total, weights, fade))
        for q_mod, refs, top, total, weights, fade in parts:
            if ready is not None:
                ready(1 - q_mod)
            mixed = None if opening else mixed_ref[h, q_mod] * fade
            for weight, (ref, _) in zip(weights, refs):
                value = jnp.concatenate(
                    [ref[VALUE, r : r + HEAD_DIM] for r in range(0, rows, HEAD_DIM)], axis=1
                )
                block = jnp.dot(value, weight, preferred_element_type=jnp.float32)
                mixed = block if mixed is None else mixed + block
            if closing:
                cols = pl.ds(pl.multiple_of(h * HEAD_DIM, HEAD_DIM), HEAD_DIM)
                out = vout if q_mod == VIDEO else aout
                out[:, cols] = jnp.transpose(mixed / total).astype(jnp.bfloat16)
            else:
                top_ref[h, q_mod] = top
                total_ref[h, q_mod] = total
                mixed_ref[h, q_mod] = mixed

    partner_copy(VALUE).wait_recv()
    partner_copy(KEY).wait_recv()

    def first_pass(h, carry):
        attend(h, (PARTNER,), opening=True)
        return carry

    lax.fori_loop(0, heads, first_pass, 0)

    start_relay(0)
    @pl.when(ahead)
    def _():
        for part in range(1, direct_parts):
            direct_copy(part).start()

    start_relay(1)
    finish_relay(0)

    def second_pass(h, carry):
        @pl.when(h + 1 < heads)
        def _():
            start_relay(h + 2)

        finish_relay(h + 1)
        attend(h, (NEAR, FAR))

        @pl.when(h >= 1)
        def _():
            last_pass(h - 1)

        return carry

    def last_pass(h):
        @pl.when(behind & (h == 0))
        def _():
            direct_copy(0).wait_recv()
            direct_copy(1).wait_recv()

        @pl.when(behind & (h >= EARLY))
        def _():
            arrived = h - EARLY + 2
            remote(
                own.at[h], far.at[DIRECT, h], direct_send.at[arrived], direct_recv.at[arrived], 2
            ).wait_recv()

        attend(h, (DIRECT,), closing=True)

    def arrive(part):
        @pl.when(behind)
        def _():
            direct_copy(part).wait_recv()

    lax.fori_loop(0, heads, second_pass, 0)

    @pl.when(lead)
    def _():
        for by in range(1, count_head):
            sum_copy(by).wait_send()
        back_copy.wait_send()

    @pl.when(jnp.logical_not(lead))
    def _():
        up_copy.wait_send()

    for kv in (KEY, VALUE):
        partner_copy(kv).wait_send()

    @pl.when(behind)
    def _():
        for part in range(heads + 1):
            for slot, mod in SPLIT:
                split_copy(slot, mod, part).wait_send()
            relay_copy(FAR, AUDIO, part).wait_send()

    @pl.when(ahead)
    def _():
        for part in range(heads + 1):
            relay_copy(NEAR, VIDEO, part).wait_send()
        for part in range(direct_parts - 1):
            direct_copy(part).wait_send()

    arrive(direct_parts - 3)
    attend(
        heads - 1,
        (DIRECT,),
        closing=True,
        ready=lambda mod: arrive(direct_parts - 2 + mod),
    )

    @pl.when(ahead)
    def _():
        direct_copy(direct_parts - 1).wait_send()


def hand_over(v_in, a_in, v_out, a_out, sems):
    parts = sems.shape[1]
    rows = v_in.shape[0] // parts
    copies = []
    for i, (src, dst) in enumerate(((v_in, v_out), (a_in, a_out))):
        for p in range(parts):
            cut = pl.ds(p * rows, rows)
            copies.append(pltpu.make_async_copy(src.at[cut], dst.at[cut], sems.at[i, p]))
    for copy in copies:
        copy.start()
    for copy in copies:
        copy.wait()


def local(
    video_q,
    video_k,
    video_v,
    audio_q,
    audio_k,
    audio_v,
    video_q_gain,
    audio_k_gain,
    audio_q_gain,
    video_k_gain,
    tile_first,
    tile_count,
):
    count_seq, count_head = lax.axis_size("seq"), lax.axis_size("head")
    rows, cols = video_q.shape
    heads = cols // HEAD_DIM

    def body(*refs):
        kernel(count_seq, count_head, *refs)

    hbm = pl.BlockSpec(memory_space=pl.ANY)
    vmem = pl.BlockSpec(memory_space=pltpu.VMEM)
    both = (jax.ShapeDtypeStruct((rows, cols), jnp.bfloat16),) * 2
    dma = pltpu.SemaphoreType.DMA
    v_out, a_out = pl.pallas_call(
        body,
        out_shape=(pltpu.VMEM((rows, cols), jnp.bfloat16),) * 2,
        in_specs=[hbm] * 12,
        out_specs=(vmem, vmem),
        scratch_shapes=[
            *[pltpu.VMEM((cols,), jnp.float32)] * 4,
            *[pltpu.SMEM((count_seq,), jnp.int32)] * 2,
            dma((6,)),
            pltpu.VMEM((4, rows, cols), jnp.bfloat16),
            pltpu.VMEM((2, rows, cols), jnp.bfloat16),
            pltpu.VMEM((heads, 2, 2, rows, HEAD_DIM), jnp.bfloat16),
            pltpu.VMEM((heads, 2, rows, HEAD_DIM), jnp.bfloat16),
            pltpu.VMEM((4, heads, 2, 2, rows, HEAD_DIM), jnp.bfloat16),
            pltpu.VMEM((heads, 2, 1, rows), jnp.float32),
            pltpu.VMEM((heads, 2, 1, rows), jnp.float32),
            pltpu.VMEM((heads, 2, HEAD_DIM, rows), jnp.float32),
            pltpu.VMEM((2, 8, rows), jnp.float32),
            pltpu.VMEM((count_head - 1, 2, 8, rows), jnp.float32),
            pltpu.VMEM((2, 8, rows), jnp.float32),
            dma((4,)),
            dma((2,)),
            dma((2,)),
            dma((2,)),
            dma((count_head - 1,)),
            dma((count_head - 1,)),
            dma((2,)),
            dma((2,)),
            dma((2, heads + 1)),
            dma((2, heads + 1)),
            dma((2, heads + 1)),
            dma((2, heads + 1)),
            dma((heads - EARLY + 4,)),
            dma((heads - EARLY + 4,)),
        ],
        compiler_params=pltpu.CompilerParams(
            collective_id=0, has_side_effects=True, vmem_limit_bytes=40 * 1024 * 1024
        ),
        name="attend",
    )(
        *(
            pltpu.with_memory_space_constraint(x, pltpu.HBM)
            for x in (
                video_q,
                video_k,
                video_v,
                audio_q,
                audio_k,
                audio_v,
                video_q_gain,
                audio_k_gain,
                audio_q_gain,
                video_k_gain,
                tile_first,
                tile_count,
            )
        )
    )
    return pl.pallas_call(
        hand_over,
        out_shape=both,
        in_specs=[vmem] * 2,
        out_specs=(hbm, hbm),
        scratch_shapes=[dma((2, 1))],
        compiler_params=pltpu.CompilerParams(vmem_limit_bytes=4 * 1024 * 1024),
        name="hand_over",
    )(*(pltpu.with_memory_space_constraint(x, pltpu.VMEM) for x in (v_out, a_out)))


def solution(mesh):
    return jax.shard_map(
        local,
        mesh=mesh,
        in_specs=(P("seq", "head"),) * 6 + (P("head"),) * 4 + (P(), P()),
        out_specs=(P("seq", "head"), P("seq", "head")),
        check_vma=False,
    )
```

```python
import jax
import jax.numpy as jnp
from jax import lax
from jax.experimental import pallas as pl
from jax.experimental.pallas import tpu as pltpu
from jax.sharding import PartitionSpec as P

HEAD_DIM = 128
EPS = 1e-06
NEG = -1e30
EARLY = 2
GROUP = 3
MESH = pl.DeviceIdType.MESH
LOG2E = 1.4426950408889634
FACTOR = LOG2E * HEAD_DIM**-0.5

PARTNER, DIRECT, NEAR, FAR = 0, 1, 2, 3
OFFSET = (1, -2, -1, 2)
AUDIO, VIDEO = 0, 1
KEY, VALUE = 0, 1
SPLIT = ((NEAR, AUDIO), (FAR, VIDEO))
RELAY = ((FAR, AUDIO), (NEAR, VIDEO))


def kernel(
    count_seq,
    count_head,
    vq_hbm,
    vk_hbm,
    vv_hbm,
    aq_hbm,
    ak_hbm,
    av_hbm,
    vqg_hbm,
    akg_hbm,
    aqg_hbm,
    vkg_hbm,
    first_hbm,
    count_hbm,
    vout,
    aout,
    vqg,
    akg,
    aqg,
    vkg,
    first_ref,
    count_ref,
    small_sem,
    raw,
    raw_v,
    own,
    nq,
    far,
    top_ref,
    total_ref,
    mixed_ref,
    sums,
    sums_in,
    all_sums,
    local_sem,
    value_sem,
    pair_send,
    pair_recv,
    sum_send,
    sum_recv,
    partner_send,
    partner_recv,
    split_send,
    split_recv,
    relay_send,
    relay_recv,
    direct_send,
    direct_recv,
):
    seq = lax.axis_index("seq")
    head = lax.axis_index("head")
    sigma = 1 - 2 * lax.rem(seq, 2)
    heads = nq.shape[0]
    rows = raw.shape[1]
    width = raw.shape[2] * count_head
    behind = (seq - sigma >= 0) & (seq - sigma < count_seq)
    ahead = (seq + 2 * sigma >= 0) & (seq + 2 * sigma < count_seq)

    loads = []
    for i, ref in enumerate((ak_hbm, vk_hbm, vq_hbm, aq_hbm)):
        loads.append(pltpu.make_async_copy(ref, raw.at[i], local_sem.at[i]))
    value_loads = [
        pltpu.make_async_copy(ref, raw_v.at[mod], value_sem.at[mod])
        for mod, ref in enumerate((av_hbm, vv_hbm))
    ]
    smalls = [
        pltpu.make_async_copy(src, dst, small_sem.at[i])
        for i, (src, dst) in enumerate(
            (
                (akg_hbm, akg),
                (vkg_hbm, vkg),
                (vqg_hbm, vqg),
                (aqg_hbm, aqg),
                (first_hbm, first_ref),
                (count_hbm, count_ref),
            )
        )
    ]
    barrier = pltpu.get_barrier_semaphore()

    def greet(by):
        pl.semaphore_signal(barrier, inc=1, device_id=(seq + by * sigma, head), device_id_type=MESH)

    @pl.when(behind)
    def _():
        greet(-1)
        greet(-2)

    @pl.when(ahead)
    def _():
        greet(2)

    greet(1)

    lead = sigma > 0

    @pl.when(lead)
    def _():
        for by in range(1, count_head):
            pl.semaphore_signal(
                barrier, inc=1, device_id=(seq, lax.rem(head + by, count_head)), device_id_type=MESH
            )

    for load in value_loads:
        load.start()
    for load in value_loads:
        load.wait()
    for h in range(heads):
        for mod in (AUDIO, VIDEO):
            for r in range(0, rows, HEAD_DIM):
                own[h, mod, VALUE, r : r + HEAD_DIM] = jnp.transpose(
                    raw_v[mod, r : r + HEAD_DIM, h * HEAD_DIM : (h + 1) * HEAD_DIM]
                )
    peers = 1 + 2 * behind.astype(jnp.int32) + ahead.astype(jnp.int32)
    peers += (count_head - 1) * lead.astype(jnp.int32)
    pl.semaphore_wait(barrier, peers)

    def remote(src, dst, send, recv, by):
        return pltpu.make_async_remote_copy(
            src_ref=src,
            dst_ref=dst,
            send_sem=send,
            recv_sem=recv,
            device_id=(seq + by * sigma, head),
            device_id_type=MESH,
        )

    def block(ref, mod, part):
        if isinstance(part, int) and part == 0:
            return ref.at[:, mod, VALUE]
        return ref.at[pl.ds((part - 1) * GROUP, GROUP), mod, KEY]

    def split_copy(slot, mod, part):
        by = -1 if slot == NEAR else -2
        return remote(
            block(own, mod, part),
            block(far.at[slot], mod, part),
            split_send.at[mod, part],
            split_recv.at[mod, part],
            by,
        )

    def relay_copy(slot, mod, part):
        held = NEAR if slot == FAR else FAR
        return remote(
            block(far.at[held], mod, part),
            block(far.at[slot], mod, part),
            relay_send.at[mod, part],
            relay_recv.at[mod, part],
            1,
        )

    def partner_copy(kv):
        return remote(own.at[:, :, kv], far.at[PARTNER, :, :, kv], partner_send.at[kv], partner_recv.at[kv], 1)

    def direct_copy(part):
        def block(ref):
            if part == 0:
                return ref.at[pl.ds(0, EARLY), :, VALUE]
            if part == 1:
                return ref.at[pl.ds(0, EARLY), :, KEY]
            if part == direct_parts - 3:
                return ref.at[heads - 1, :, KEY]
            if part >= direct_parts - 2:
                return ref.at[heads - 1, part - direct_parts + 2, VALUE]
            return ref.at[part - 2 + EARLY]

        return remote(
            block(own), block(far.at[DIRECT]), direct_send.at[part], direct_recv.at[part], 2
        )

    direct_parts = heads - EARLY + 4

    def start_split(part):
        @pl.when(behind)
        def _():
            for slot, mod in SPLIT:
                split_copy(slot, mod, part).start()

    def start_relay(part):
        @pl.when(behind)
        def _():
            split_copy(NEAR, AUDIO, part).wait_recv()
            relay_copy(FAR, AUDIO, part).start()

        @pl.when(ahead)
        def _():
            split_copy(FAR, VIDEO, part).wait_recv()
            relay_copy(NEAR, VIDEO, part).start()

    def finish_relay(part):
        @pl.when(ahead)
        def _():
            relay_copy(FAR, AUDIO, part).wait_recv()

        @pl.when(behind)
        def _():
            relay_copy(NEAR, VIDEO, part).wait_recv()

    start_split(0)

    @pl.when(ahead)
    def _():
        direct_copy(0).start()

    partner_copy(VALUE).start()
    for load in loads + smalls:
        load.start()

    def clear(slot):
        def body(h, carry):
            far[slot, h] = jnp.zeros(far.shape[2:], far.dtype)
            return carry

        lax.fori_loop(0, heads, body, 0)

    @pl.when(jnp.logical_not(behind))
    def _():
        clear(DIRECT)
        clear(NEAR)

    @pl.when(jnp.logical_not(ahead))
    def _():
        clear(FAR)

    lane = lax.broadcasted_iota(jnp.int32, (rows, HEAD_DIM), 1)
    packed = jnp.zeros((rows, HEAD_DIM), jnp.float32)
    for i in range(4):
        loads[i].wait()
        total = jnp.zeros((rows, HEAD_DIM), jnp.float32)
        for h in range(heads):
            wide = raw[i, :, h * HEAD_DIM : (h + 1) * HEAD_DIM].astype(jnp.float32)
            total += wide * wide
        packed = jnp.where(lane == i, jnp.sum(total, axis=1, keepdims=True), packed)
    for load in smalls:
        load.wait()
    core = lax.rem(seq, 2)
    sums[core] = jnp.transpose(packed)[:8]

    def sum_copy(by):
        return pltpu.make_async_remote_copy(
            src_ref=sums,
            dst_ref=sums_in.at[by - 1],
            send_sem=sum_send.at[by - 1],
            recv_sem=sum_recv.at[by - 1],
            device_id=(seq, lax.rem(head + by, count_head)),
            device_id_type=MESH,
        )

    up_copy = remote(sums.at[1], sums.at[1], pair_send.at[0], pair_recv.at[0], 1)
    back_copy = remote(all_sums.at[1], all_sums.at[1], pair_send.at[1], pair_recv.at[1], 1)

    @pl.when(lead)
    def _():
        up_copy.wait_recv()
        for by in range(1, count_head):
            sum_copy(by).start()
        total = sums[...]
        for by in range(1, count_head):
            sum_copy(by).wait_recv()
            total += sums_in[by - 1]
        all_sums[...] = total
        back_copy.start()

    @pl.when(jnp.logical_not(lead))
    def _():
        up_copy.start()
        back_copy.wait_recv()

    scale = lax.rsqrt(all_sums[core] / width + EPS)
    scale = jnp.transpose(jnp.concatenate([scale] * (HEAD_DIM // 8), axis=0))

    def normalized(i, gain, h):
        cols = slice(h * HEAD_DIM, (h + 1) * HEAD_DIM)
        wide = raw[i, :, cols].astype(jnp.float32)
        return (wide * scale[:, i : i + 1] * gain[cols]).astype(jnp.bfloat16)

    for h in range(heads):
        own[h, AUDIO, KEY] = normalized(0, akg, h)
        own[h, VIDEO, KEY] = normalized(1, vkg, h)
        if h % GROUP == GROUP - 1:
            start_split(h // GROUP + 1)

    partner_copy(KEY).start()
    for h in range(heads):
        nq[h, VIDEO] = normalized(2, vqg, h)
        nq[h, AUDIO] = normalized(3, aqg, h)

    def covers(stretch, tile):
        safe = lax.rem(stretch + count_seq, count_seq)
        first = first_ref[safe]
        inside = (stretch >= 0) & (stretch < count_seq) & (tile >= 0) & (tile < count_seq)
        return inside & (tile >= first) & (tile < first + count_ref[safe])

    bias = ([], [])
    for slot in range(4):
        other = seq + OFFSET[slot] * sigma
        bias[VIDEO].append(jnp.where(covers(other, seq), 0.0, NEG))
        bias[AUDIO].append(jnp.where(covers(seq, other), 0.0, NEG))

    def attend(h, slots, opening=False, closing=False, ready=None):
        jobs = []
        for q_mod in (VIDEO, AUDIO):
            refs = [(far.at[slot, h, 1 - q_mod], bias[q_mod][slot]) for slot in slots]
            if opening:
                refs.insert(0, (own.at[h, 1 - q_mod], 0.0))
            query = nq[h, q_mod]
            scores = [
                lax.dot_general(
                    ref[KEY], query, (((1,), (1,)), ((), ())), preferred_element_type=jnp.float32
                )
                for ref, _ in refs
            ]
            jobs.append((q_mod, refs, scores))
        tops = []
        for q_mod, refs, scores in jobs:
            top = None if opening else top_ref[h, q_mod]
            for score, (_, add) in zip(scores, refs):
                most = jnp.max(score, axis=0, keepdims=True) + add
                top = most if top is None else jnp.maximum(top, most)
            tops.append(top)
        parts = []
        for (q_mod, refs, scores), top in zip(jobs, tops):
            total, weights = None, []
            for score, (_, add) in zip(scores, refs):
                weight = jnp.exp2((score - (top - add)) * FACTOR)
                part = jnp.sum(weight, axis=0, keepdims=True)
                total = part if total is None else total + part
                weights.append(weight.astype(jnp.bfloat16))
            fade = None
            if not opening:
                fade = jnp.exp2((top_ref[h, q_mod] - top) * FACTOR)
                total += total_ref[h, q_mod] * fade
            parts.append((q_mod, refs, top, total, weights, fade))
        for q_mod, refs, top, total, weights, fade in parts:
            if ready is not None:
                ready(1 - q_mod)
            mixed = None if opening else mixed_ref[h, q_mod] * fade
            for weight, (ref, _) in zip(weights, refs):
                value = jnp.concatenate(
                    [ref[VALUE, r : r + HEAD_DIM] for r in range(0, rows, HEAD_DIM)], axis=1
                )
                block = jnp.dot(value, weight, preferred_element_type=jnp.float32)
                mixed = block if mixed is None else mixed + block
            if closing:
                cols = pl.ds(pl.multiple_of(h * HEAD_DIM, HEAD_DIM), HEAD_DIM)
                out = vout if q_mod == VIDEO else aout
                out[:, cols] = jnp.transpose(mixed / total).astype(jnp.bfloat16)
            else:
                top_ref[h, q_mod] = top
                total_ref[h, q_mod] = total
                mixed_ref[h, q_mod] = mixed

    partner_copy(VALUE).wait_recv()
    partner_copy(KEY).wait_recv()

    def first_pass(h, carry):
        attend(h, (PARTNER,), opening=True)
        return carry

    lax.fori_loop(0, heads, first_pass, 0)

    start_relay(0)
    @pl.when(ahead)
    def _():
        for part in range(1, direct_parts):
            direct_copy(part).start()

    start_relay(1)
    finish_relay(0)

    def second_pass(h, carry):
        part = h // GROUP + 1

        @pl.when((lax.rem(h, GROUP) == 0) & (h + GROUP < heads))
        def _():
            start_relay(part + 1)

        @pl.when(lax.rem(h, GROUP) == 0)
        def _():
            finish_relay(part)

        attend(h, (NEAR, FAR))

        @pl.when(h >= 1)
        def _():
            last_pass(h - 1)

        return carry

    def last_pass(h):
        @pl.when(behind & (h == 0))
        def _():
            direct_copy(0).wait_recv()
            direct_copy(1).wait_recv()

        @pl.when(behind & (h >= EARLY))
        def _():
            arrived = h - EARLY + 2
            remote(
                own.at[h], far.at[DIRECT, h], direct_send.at[arrived], direct_recv.at[arrived], 2
            ).wait_recv()

        attend(h, (DIRECT,), closing=True)

    def arrive(part):
        @pl.when(behind)
        def _():
            direct_copy(part).wait_recv()

    lax.fori_loop(0, heads, second_pass, 0)

    @pl.when(lead)
    def _():
        for by in range(1, count_head):
            sum_copy(by).wait_send()
        back_copy.wait_send()

    @pl.when(jnp.logical_not(lead))
    def _():
        up_copy.wait_send()

    for kv in (KEY, VALUE):
        partner_copy(kv).wait_send()

    @pl.when(behind)
    def _():
        for part in range(heads // GROUP + 1):
            for slot, mod in SPLIT:
                split_copy(slot, mod, part).wait_send()
            relay_copy(FAR, AUDIO, part).wait_send()

    @pl.when(ahead)
    def _():
        for part in range(heads // GROUP + 1):
            relay_copy(NEAR, VIDEO, part).wait_send()
        for part in range(direct_parts - 1):
            direct_copy(part).wait_send()

    arrive(direct_parts - 3)
    attend(
        heads - 1,
        (DIRECT,),
        closing=True,
        ready=lambda mod: arrive(direct_parts - 2 + mod),
    )

    @pl.when(ahead)
    def _():
        direct_copy(direct_parts - 1).wait_send()


def hand_over(v_in, a_in, v_out, a_out, sems):
    parts = sems.shape[1]
    rows = v_in.shape[0] // parts
    copies = []
    for i, (src, dst) in enumerate(((v_in, v_out), (a_in, a_out))):
        for p in range(parts):
            cut = pl.ds(p * rows, rows)
            copies.append(pltpu.make_async_copy(src.at[cut], dst.at[cut], sems.at[i, p]))
    for copy in copies:
        copy.start()
    for copy in copies:
        copy.wait()


def local(
    video_q,
    video_k,
    video_v,
    audio_q,
    audio_k,
    audio_v,
    video_q_gain,
    audio_k_gain,
    audio_q_gain,
    video_k_gain,
    tile_first,
    tile_count,
):
    count_seq, count_head = lax.axis_size("seq"), lax.axis_size("head")
    rows, cols = video_q.shape
    heads = cols // HEAD_DIM

    def body(*refs):
        kernel(count_seq, count_head, *refs)

    hbm = pl.BlockSpec(memory_space=pl.ANY)
    vmem = pl.BlockSpec(memory_space=pltpu.VMEM)
    both = (jax.ShapeDtypeStruct((rows, cols), jnp.bfloat16),) * 2
    dma = pltpu.SemaphoreType.DMA
    v_out, a_out = pl.pallas_call(
        body,
        out_shape=(pltpu.VMEM((rows, cols), jnp.bfloat16),) * 2,
        in_specs=[hbm] * 12,
        out_specs=(vmem, vmem),
        scratch_shapes=[
            *[pltpu.VMEM((cols,), jnp.float32)] * 4,
            *[pltpu.SMEM((count_seq,), jnp.int32)] * 2,
            dma((6,)),
            pltpu.VMEM((4, rows, cols), jnp.bfloat16),
            pltpu.VMEM((2, rows, cols), jnp.bfloat16),
            pltpu.VMEM((heads, 2, 2, rows, HEAD_DIM), jnp.bfloat16),
            pltpu.VMEM((heads, 2, rows, HEAD_DIM), jnp.bfloat16),
            pltpu.VMEM((4, heads, 2, 2, rows, HEAD_DIM), jnp.bfloat16),
            pltpu.VMEM((heads, 2, 1, rows), jnp.float32),
            pltpu.VMEM((heads, 2, 1, rows), jnp.float32),
            pltpu.VMEM((heads, 2, HEAD_DIM, rows), jnp.float32),
            pltpu.VMEM((2, 8, rows), jnp.float32),
            pltpu.VMEM((count_head - 1, 2, 8, rows), jnp.float32),
            pltpu.VMEM((2, 8, rows), jnp.float32),
            dma((4,)),
            dma((2,)),
            dma((2,)),
            dma((2,)),
            dma((count_head - 1,)),
            dma((count_head - 1,)),
            dma((2,)),
            dma((2,)),
            dma((2, heads // GROUP + 1)),
            dma((2, heads // GROUP + 1)),
            dma((2, heads // GROUP + 1)),
            dma((2, heads // GROUP + 1)),
            dma((heads - EARLY + 4,)),
            dma((heads - EARLY + 4,)),
        ],
        compiler_params=pltpu.CompilerParams(
            collective_id=0, has_side_effects=True, vmem_limit_bytes=40 * 1024 * 1024
        ),
        name="attend",
    )(
        *(
            pltpu.with_memory_space_constraint(x, pltpu.HBM)
            for x in (
                video_q,
                video_k,
                video_v,
                audio_q,
                audio_k,
                audio_v,
                video_q_gain,
                audio_k_gain,
                audio_q_gain,
                video_k_gain,
                tile_first,
                tile_count,
            )
        )
    )
    return pl.pallas_call(
        hand_over,
        out_shape=both,
        in_specs=[vmem] * 2,
        out_specs=(hbm, hbm),
        scratch_shapes=[dma((2, 1))],
        compiler_params=pltpu.CompilerParams(vmem_limit_bytes=4 * 1024 * 1024),
        name="hand_over",
    )(*(pltpu.with_memory_space_constraint(x, pltpu.VMEM) for x in (v_out, a_out)))


def solution(mesh):
    return jax.shard_map(
        local,
        mesh=mesh,
        in_specs=(P("seq", "head"),) * 6 + (P("head"),) * 4 + (P(), P()),
        out_specs=(P("seq", "head"), P("seq", "head")),
        check_vma=False,
    )
```

```python
import jax
import jax.numpy as jnp
from jax import lax
from jax.experimental import pallas as pl
from jax.experimental.pallas import tpu as pltpu
from jax.sharding import PartitionSpec as P

HEAD_DIM = 128
EPS = 1e-06
NEG = -1e30
EARLY = 2
GROUP = 3
MESH = pl.DeviceIdType.MESH
LOG2E = 1.4426950408889634
FACTOR = LOG2E * HEAD_DIM**-0.5

PARTNER, DIRECT, NEAR, FAR = 0, 1, 2, 3
OFFSET = (1, -2, -1, 2)
AUDIO, VIDEO = 0, 1
KEY, VALUE = 0, 1
SPLIT = ((NEAR, AUDIO), (FAR, VIDEO))
RELAY = ((FAR, AUDIO), (NEAR, VIDEO))


def kernel(
    count_seq,
    count_head,
    vq_hbm,
    vk_hbm,
    vv_hbm,
    aq_hbm,
    ak_hbm,
    av_hbm,
    vqg_hbm,
    akg_hbm,
    aqg_hbm,
    vkg_hbm,
    first_hbm,
    count_hbm,
    vout,
    aout,
    vqg,
    akg,
    aqg,
    vkg,
    first_ref,
    count_ref,
    small_sem,
    raw,
    raw_v,
    own,
    nq,
    far,
    top_ref,
    total_ref,
    mixed_ref,
    sums,
    sums_in,
    all_sums,
    local_sem,
    value_sem,
    pair_send,
    pair_recv,
    sum_send,
    sum_recv,
    partner_send,
    partner_recv,
    split_send,
    split_recv,
    relay_send,
    relay_recv,
    direct_send,
    direct_recv,
):
    seq = lax.axis_index("seq")
    head = lax.axis_index("head")
    sigma = 1 - 2 * lax.rem(seq, 2)
    heads = nq.shape[0]
    rows = raw.shape[1]
    width = raw.shape[2] * count_head
    behind = (seq - sigma >= 0) & (seq - sigma < count_seq)
    ahead = (seq + 2 * sigma >= 0) & (seq + 2 * sigma < count_seq)

    loads = []
    for i, ref in enumerate((ak_hbm, vk_hbm, vq_hbm, aq_hbm)):
        loads.append(pltpu.make_async_copy(ref, raw.at[i], local_sem.at[i]))
    value_loads = [
        pltpu.make_async_copy(ref, raw_v.at[mod], value_sem.at[mod])
        for mod, ref in enumerate((av_hbm, vv_hbm))
    ]
    smalls = [
        pltpu.make_async_copy(src, dst, small_sem.at[i])
        for i, (src, dst) in enumerate(
            (
                (akg_hbm, akg),
                (vkg_hbm, vkg),
                (vqg_hbm, vqg),
                (aqg_hbm, aqg),
                (first_hbm, first_ref),
                (count_hbm, count_ref),
            )
        )
    ]
    barrier = pltpu.get_barrier_semaphore()

    def greet(by):
        pl.semaphore_signal(barrier, inc=1, device_id=(seq + by * sigma, head), device_id_type=MESH)

    @pl.when(behind)
    def _():
        greet(-1)
        greet(-2)

    @pl.when(ahead)
    def _():
        greet(2)

    greet(1)

    lead = sigma > 0

    @pl.when(lead)
    def _():
        for by in range(1, count_head):
            pl.semaphore_signal(
                barrier, inc=1, device_id=(seq, lax.rem(head + by, count_head)), device_id_type=MESH
            )

    for load in value_loads:
        load.start()
    for load in value_loads:
        load.wait()
    for h in range(heads):
        for mod in (AUDIO, VIDEO):
            for r in range(0, rows, HEAD_DIM):
                own[h, mod, VALUE, r : r + HEAD_DIM] = jnp.transpose(
                    raw_v[mod, r : r + HEAD_DIM, h * HEAD_DIM : (h + 1) * HEAD_DIM]
                )
    peers = 1 + 2 * behind.astype(jnp.int32) + ahead.astype(jnp.int32)
    peers += (count_head - 1) * lead.astype(jnp.int32)
    pl.semaphore_wait(barrier, peers)

    def remote(src, dst, send, recv, by):
        return pltpu.make_async_remote_copy(
            src_ref=src,
            dst_ref=dst,
            send_sem=send,
            recv_sem=recv,
            device_id=(seq + by * sigma, head),
            device_id_type=MESH,
        )

    def block(ref, mod, part):
        if isinstance(part, int) and part == 0:
            return ref.at[:, mod, VALUE]
        return ref.at[pl.ds((part - 1) * GROUP, GROUP), mod, KEY]

    def split_copy(slot, mod, part):
        by = -1 if slot == NEAR else -2
        return remote(
            block(own, mod, part),
            block(far.at[slot], mod, part),
            split_send.at[mod, part],
            split_recv.at[mod, part],
            by,
        )

    def relay_copy(slot, mod, part):
        held = NEAR if slot == FAR else FAR
        return remote(
            block(far.at[held], mod, part),
            block(far.at[slot], mod, part),
            relay_send.at[mod, part],
            relay_recv.at[mod, part],
            1,
        )

    def partner_copy(kv):
        return remote(own.at[:, :, kv], far.at[PARTNER, :, :, kv], partner_send.at[kv], partner_recv.at[kv], 1)

    def direct_copy(part):
        def block(ref):
            if part == 0:
                return ref.at[pl.ds(0, EARLY), :, VALUE]
            if part == 1:
                return ref.at[pl.ds(0, EARLY), :, KEY]
            if part == direct_parts - 3:
                return ref.at[heads - 1, :, KEY]
            if part >= direct_parts - 2:
                return ref.at[heads - 1, part - direct_parts + 2, VALUE]
            return ref.at[part - 2 + EARLY]

        return remote(
            block(own), block(far.at[DIRECT]), direct_send.at[part], direct_recv.at[part], 2
        )

    direct_parts = heads - EARLY + 4

    def start_split(part):
        @pl.when(behind)
        def _():
            for slot, mod in SPLIT:
                split_copy(slot, mod, part).start()

    def start_relay(part):
        @pl.when(behind)
        def _():
            split_copy(NEAR, AUDIO, part).wait_recv()
            relay_copy(FAR, AUDIO, part).start()

        @pl.when(ahead)
        def _():
            split_copy(FAR, VIDEO, part).wait_recv()
            relay_copy(NEAR, VIDEO, part).start()

    def finish_relay(part):
        @pl.when(ahead)
        def _():
            relay_copy(FAR, AUDIO, part).wait_recv()

        @pl.when(behind)
        def _():
            relay_copy(NEAR, VIDEO, part).wait_recv()

    start_split(0)

    @pl.when(ahead)
    def _():
        direct_copy(0).start()

    partner_copy(VALUE).start()
    for load in loads + smalls:
        load.start()

    def clear(slot):
        def body(h, carry):
            far[slot, h] = jnp.zeros(far.shape[2:], far.dtype)
            return carry

        lax.fori_loop(0, heads, body, 0)

    @pl.when(jnp.logical_not(behind))
    def _():
        clear(DIRECT)
        clear(NEAR)

    @pl.when(jnp.logical_not(ahead))
    def _():
        clear(FAR)

    lane = lax.broadcasted_iota(jnp.int32, (rows, HEAD_DIM), 1)
    packed = jnp.zeros((rows, HEAD_DIM), jnp.float32)
    for i in range(4):
        loads[i].wait()
        total = jnp.zeros((rows, HEAD_DIM), jnp.float32)
        for h in range(heads):
            wide = raw[i, :, h * HEAD_DIM : (h + 1) * HEAD_DIM].astype(jnp.float32)
            total += wide * wide
        packed = jnp.where(lane == i, jnp.sum(total, axis=1, keepdims=True), packed)
    for load in smalls:
        load.wait()
    core = lax.rem(seq, 2)
    sums[core] = jnp.transpose(packed)[:8]

    def sum_copy(by):
        return pltpu.make_async_remote_copy(
            src_ref=sums,
            dst_ref=sums_in.at[by - 1],
            send_sem=sum_send.at[by - 1],
            recv_sem=sum_recv.at[by - 1],
            device_id=(seq, lax.rem(head + by, count_head)),
            device_id_type=MESH,
        )

    up_copy = remote(sums.at[1], sums.at[1], pair_send.at[0], pair_recv.at[0], 1)
    back_copy = remote(all_sums.at[1], all_sums.at[1], pair_send.at[1], pair_recv.at[1], 1)

    @pl.when(lead)
    def _():
        up_copy.wait_recv()
        for by in range(1, count_head):
            sum_copy(by).start()
        total = sums[...]
        for by in range(1, count_head):
            sum_copy(by).wait_recv()
            total += sums_in[by - 1]
        all_sums[...] = total
        back_copy.start()

    @pl.when(jnp.logical_not(lead))
    def _():
        up_copy.start()
        back_copy.wait_recv()

    scale = lax.rsqrt(all_sums[core] / width + EPS)
    scale = jnp.transpose(jnp.concatenate([scale] * (HEAD_DIM // 8), axis=0))

    def normalized(i, gain, h):
        cols = slice(h * HEAD_DIM, (h + 1) * HEAD_DIM)
        wide = raw[i, :, cols].astype(jnp.float32)
        return (wide * scale[:, i : i + 1] * gain[cols]).astype(jnp.bfloat16)

    for h in range(heads):
        own[h, AUDIO, KEY] = normalized(0, akg, h)
        own[h, VIDEO, KEY] = normalized(1, vkg, h)
        if h % GROUP == GROUP - 1:
            start_split(h // GROUP + 1)

    partner_copy(KEY).start()
    for h in range(heads):
        nq[h, VIDEO] = normalized(2, vqg, h)
        nq[h, AUDIO] = normalized(3, aqg, h)

    def covers(stretch, tile):
        safe = lax.rem(stretch + count_seq, count_seq)
        first = first_ref[safe]
        inside = (stretch >= 0) & (stretch < count_seq) & (tile >= 0) & (tile < count_seq)
        return inside & (tile >= first) & (tile < first + count_ref[safe])

    bias = ([], [])
    for slot in range(4):
        other = seq + OFFSET[slot] * sigma
        bias[VIDEO].append(jnp.where(covers(other, seq), 0.0, NEG))
        bias[AUDIO].append(jnp.where(covers(seq, other), 0.0, NEG))

    def attend(h, slots, opening=False, closing=False, ready=None):
        jobs = []
        for q_mod in (VIDEO, AUDIO):
            refs = [(far.at[slot, h, 1 - q_mod], bias[q_mod][slot]) for slot in slots]
            if opening:
                refs.insert(0, (own.at[h, 1 - q_mod], 0.0))
            query = nq[h, q_mod]
            scores = [
                lax.dot_general(
                    ref[KEY], query, (((1,), (1,)), ((), ())), preferred_element_type=jnp.float32
                )
                for ref, _ in refs
            ]
            jobs.append((q_mod, refs, scores))
        tops = []
        for q_mod, refs, scores in jobs:
            top = None if opening else top_ref[h, q_mod]
            for score, (_, add) in zip(scores, refs):
                most = jnp.max(score, axis=0, keepdims=True) + add
                top = most if top is None else jnp.maximum(top, most)
            tops.append(top)
        parts = []
        for (q_mod, refs, scores), top in zip(jobs, tops):
            total, weights = None, []
            for score, (_, add) in zip(scores, refs):
                weight = jnp.exp2((score - (top - add)) * FACTOR)
                part = jnp.sum(weight, axis=0, keepdims=True)
                total = part if total is None else total + part
                weights.append(weight.astype(jnp.bfloat16))
            fade = None
            if not opening:
                fade = jnp.exp2((top_ref[h, q_mod] - top) * FACTOR)
                total += total_ref[h, q_mod] * fade
            mixed = None if opening else mixed_ref[h, q_mod] * fade
            share = None
            if closing:
                share = 1.0 / total
                mixed *= share
            parts.append((q_mod, refs, top, total, weights, mixed, share))
        for q_mod, refs, top, total, weights, mixed, share in parts:
            if ready is not None:
                ready(1 - q_mod)
            for weight, (ref, _) in zip(weights, refs):
                value = jnp.concatenate(
                    [ref[VALUE, r : r + HEAD_DIM] for r in range(0, rows, HEAD_DIM)], axis=1
                )
                block = jnp.dot(value, weight, preferred_element_type=jnp.float32)
                if closing:
                    block *= share
                mixed = block if mixed is None else mixed + block
            if closing:
                cols = pl.ds(pl.multiple_of(h * HEAD_DIM, HEAD_DIM), HEAD_DIM)
                out = vout if q_mod == VIDEO else aout
                out[:, cols] = jnp.transpose(mixed.astype(jnp.bfloat16))
            else:
                top_ref[h, q_mod] = top
                total_ref[h, q_mod] = total
                mixed_ref[h, q_mod] = mixed

    partner_copy(VALUE).wait_recv()
    partner_copy(KEY).wait_recv()

    def first_pass(h, carry):
        attend(h, (PARTNER,), opening=True)
        return carry

    lax.fori_loop(0, heads, first_pass, 0)

    start_relay(0)
    @pl.when(ahead)
    def _():
        for part in range(1, direct_parts):
            direct_copy(part).start()

    start_relay(1)
    finish_relay(0)

    def second_pass(h, carry):
        part = h // GROUP + 1

        @pl.when((lax.rem(h, GROUP) == 0) & (h + GROUP < heads))
        def _():
            start_relay(part + 1)

        @pl.when(lax.rem(h, GROUP) == 0)
        def _():
            finish_relay(part)

        attend(h, (NEAR, FAR))

        @pl.when(h >= 1)
        def _():
            last_pass(h - 1)

        return carry

    def last_pass(h):
        @pl.when(behind & (h == 0))
        def _():
            direct_copy(0).wait_recv()
            direct_copy(1).wait_recv()

        @pl.when(behind & (h >= EARLY))
        def _():
            arrived = h - EARLY + 2
            remote(
                own.at[h], far.at[DIRECT, h], direct_send.at[arrived], direct_recv.at[arrived], 2
            ).wait_recv()

        attend(h, (DIRECT,), closing=True)

    def arrive(part):
        @pl.when(behind)
        def _():
            direct_copy(part).wait_recv()

    lax.fori_loop(0, heads, second_pass, 0)

    @pl.when(lead)
    def _():
        for by in range(1, count_head):
            sum_copy(by).wait_send()
        back_copy.wait_send()

    @pl.when(jnp.logical_not(lead))
    def _():
        up_copy.wait_send()

    for kv in (KEY, VALUE):
        partner_copy(kv).wait_send()

    @pl.when(behind)
    def _():
        for part in range(heads // GROUP + 1):
            for slot, mod in SPLIT:
                split_copy(slot, mod, part).wait_send()
            relay_copy(FAR, AUDIO, part).wait_send()

    @pl.when(ahead)
    def _():
        for part in range(heads // GROUP + 1):
            relay_copy(NEAR, VIDEO, part).wait_send()
        for part in range(direct_parts - 1):
            direct_copy(part).wait_send()

    arrive(direct_parts - 3)
    attend(
        heads - 1,
        (DIRECT,),
        closing=True,
        ready=lambda mod: arrive(direct_parts - 2 + mod),
    )

    @pl.when(ahead)
    def _():
        direct_copy(direct_parts - 1).wait_send()


def hand_over(v_in, a_in, v_out, a_out, sems):
    parts = sems.shape[1]
    rows = v_in.shape[0] // parts
    copies = []
    for i, (src, dst) in enumerate(((v_in, v_out), (a_in, a_out))):
        for p in range(parts):
            cut = pl.ds(p * rows, rows)
            copies.append(pltpu.make_async_copy(src.at[cut], dst.at[cut], sems.at[i, p]))
    for copy in copies:
        copy.start()
    for copy in copies:
        copy.wait()


def local(
    video_q,
    video_k,
    video_v,
    audio_q,
    audio_k,
    audio_v,
    video_q_gain,
    audio_k_gain,
    audio_q_gain,
    video_k_gain,
    tile_first,
    tile_count,
):
    count_seq, count_head = lax.axis_size("seq"), lax.axis_size("head")
    rows, cols = video_q.shape
    heads = cols // HEAD_DIM

    def body(*refs):
        kernel(count_seq, count_head, *refs)

    hbm = pl.BlockSpec(memory_space=pl.ANY)
    vmem = pl.BlockSpec(memory_space=pltpu.VMEM)
    both = (jax.ShapeDtypeStruct((rows, cols), jnp.bfloat16),) * 2
    dma = pltpu.SemaphoreType.DMA
    v_out, a_out = pl.pallas_call(
        body,
        out_shape=(pltpu.VMEM((rows, cols), jnp.bfloat16),) * 2,
        in_specs=[hbm] * 12,
        out_specs=(vmem, vmem),
        scratch_shapes=[
            *[pltpu.VMEM((cols,), jnp.float32)] * 4,
            *[pltpu.SMEM((count_seq,), jnp.int32)] * 2,
            dma((6,)),
            pltpu.VMEM((4, rows, cols), jnp.bfloat16),
            pltpu.VMEM((2, rows, cols), jnp.bfloat16),
            pltpu.VMEM((heads, 2, 2, rows, HEAD_DIM), jnp.bfloat16),
            pltpu.VMEM((heads, 2, rows, HEAD_DIM), jnp.bfloat16),
            pltpu.VMEM((4, heads, 2, 2, rows, HEAD_DIM), jnp.bfloat16),
            pltpu.VMEM((heads, 2, 1, rows), jnp.float32),
            pltpu.VMEM((heads, 2, 1, rows), jnp.float32),
            pltpu.VMEM((heads, 2, HEAD_DIM, rows), jnp.float32),
            pltpu.VMEM((2, 8, rows), jnp.float32),
            pltpu.VMEM((count_head - 1, 2, 8, rows), jnp.float32),
            pltpu.VMEM((2, 8, rows), jnp.float32),
            dma((4,)),
            dma((2,)),
            dma((2,)),
            dma((2,)),
            dma((count_head - 1,)),
            dma((count_head - 1,)),
            dma((2,)),
            dma((2,)),
            dma((2, heads // GROUP + 1)),
            dma((2, heads // GROUP + 1)),
            dma((2, heads // GROUP + 1)),
            dma((2, heads // GROUP + 1)),
            dma((heads - EARLY + 4,)),
            dma((heads - EARLY + 4,)),
        ],
        compiler_params=pltpu.CompilerParams(
            collective_id=0, has_side_effects=True, vmem_limit_bytes=40 * 1024 * 1024
        ),
        name="attend",
    )(
        *(
            pltpu.with_memory_space_constraint(x, pltpu.HBM)
            for x in (
                video_q,
                video_k,
                video_v,
                audio_q,
                audio_k,
                audio_v,
                video_q_gain,
                audio_k_gain,
                audio_q_gain,
                video_k_gain,
                tile_first,
                tile_count,
            )
        )
    )
    return pl.pallas_call(
        hand_over,
        out_shape=both,
        in_specs=[vmem] * 2,
        out_specs=(hbm, hbm),
        scratch_shapes=[dma((2, 1))],
        compiler_params=pltpu.CompilerParams(vmem_limit_bytes=4 * 1024 * 1024),
        name="hand_over",
    )(*(pltpu.with_memory_space_constraint(x, pltpu.VMEM) for x in (v_out, a_out)))


def solution(mesh):
    return jax.shard_map(
        local,
        mesh=mesh,
        in_specs=(P("seq", "head"),) * 6 + (P("head"),) * 4 + (P(), P()),
        out_specs=(P("seq", "head"), P("seq", "head")),
        check_vma=False,
    )
```
